512 devices in a mesh: section: 16 (over z_lo, core), expert: 8 (over y, z_hi), dp: 4 (over x).
Axes of the slice: x: 4, y: 4, z: 16 (z_hi: 2, z_lo: 8; z = z_hi * 8 + z_lo), core: 2. Of those that a mesh axis runs over, the one named last changes fastest.
Arguments:
- tokens: bfloat16 [65536, 3072], P(('section', 'expert', 'dp')), parts along dimension 0, may hold values from -6 to 6
- expert_ids: int32 [65536, 2], P(('section', 'expert', 'dp')), parts along dimension 0, may hold values from 0 to 7, all different within a row; in each aligned block of 128 rows (0 to 127, 128 to 255, ...) at most 64 rows name the same one
- gate_scores: float32 [65536, 2], P(('section', 'expert', 'dp')), parts along dimension 0, may hold values from 0.1 to 1
- gate_weight: bfloat16 [128, 3072, 128], P(('section', 'expert'), 'dp'), parts along dimension 0, may hold values from -0.109375 to 0.109375
- up_weight: bfloat16 [128, 3072, 128], P(('section', 'expert'), 'dp'), parts along dimension 0, may hold values from -0.109375 to 0.109375
- down_weight: bfloat16 [128, 3072, 128], P(('section', 'expert'), 'dp'), parts along dimension 0, may hold values from -0.5 to 0.5
- grad_out: bfloat16 [65536, 3072], P(('section', 'expert', 'dp')), parts along dimension 0, may hold values from -6 to 6
Outputs:
- layer_out: bfloat16 [65536, 3072], P(('section', 'expert', 'dp')), parts along dimension 0
- grad_tokens: bfloat16 [65536, 3072], P(('section', 'expert', 'dp')), parts along dimension 0
- grad_scores: float32 [65536, 2], P(('section', 'expert', 'dp')), parts along dimension 0
- grad_gate_weight: float32 [128, 3072, 128], P(('section', 'expert'), 'dp'), parts along dimension 0
- grad_up_weight: float32 [128, 3072, 128], P(('section', 'expert'), 'dp'), parts along dimension 0
- grad_down_weight: float32 [128, 3072, 128], P(('section', 'expert'), 'dp'), parts along dimension 0
The draws below stay inside these ranges and needn't reach their ends.
There are 16 independent parts, one for each index of `section`. The reference program is written for one: setup_inputs(seed, part) draws one part's arguments, and reference() takes and returns one part's arrays. A program takes and returns all parts, laid end to end along the dimension named above; each array names one. Nothing has to cross between parts.
Inputs may be any that keep to these rules, and one draw needn't show every extreme that they name: `expert_ids`: each token names 2 different experts. In each aligned block of 128 rows (the rows of one device) no expert is named by more than 64 rows, and in some blocks an expert is named by exactly 64 rows.
All inputs are finite; a program needn't handle non-finite values.
Results may differ from the reference program's by a relative error of at most 0.012.
Values may be sent and summed in bfloat16 or wider, within the bound.
A program may use at most 64 MiB of HBM per device.

```python
import math
import jax
import jax.numpy as jnp
import numpy as np
from jax import lax

D = 3072
F = 128
EXPERTS = 8
TOP = 2
TOK_DEV = 128
CAP = 64
TOKENS = 4096
N_DP = 4


def shard_levels(rng, extent, shards, smallest, largest):
    def one(dim, parts):
        steps = jax.random.uniform(jax.random.fold_in(jax.random.fold_in(rng, 6), dim), (parts,), jnp.float32, smallest / len(shards), largest / len(shards))
        return jnp.repeat(jnp.exp(steps), extent[dim] // parts).reshape((-1,) + (1,) * (len(extent) - dim - 1))

    factor_of = one(*shards[0])
    for cut in shards[1:]:
        factor_of = factor_of * one(*cut)
    return factor_of


def shared_out(own_key, own, number, rows, count, top, bound, slope):
    sequence = jax.random.permutation(own_key, count)
    crowded, common = portions_of(count, rows * top, bound, slope, True), portions_of(count, rows * top, bound, slope, False)
    places = jnp.arange(count)

    def named(sizes, offset_by):
        used = int((sizes > 0).sum())
        fixed = max(1, used // 4)
        passed = fixed + (places - fixed + offset_by * (used - fixed)) % max(1, count - fixed)
        return jnp.zeros((count,), jnp.int32).at[sequence[jnp.where(places < fixed, places, passed)]].set(jnp.asarray(sizes, jnp.int32))

    sizes = jnp.where(number % 4 == 0, named(crowded, number // 4), named(common, number - number // 4 - 1))
    mixed = jax.random.permutation(jax.random.fold_in(own, 3), count)
    giver, taker = mixed[0:count // 2 * 2:2], mixed[1:count // 2 * 2:2]
    room = jnp.minimum(sizes[giver] - 1, bound - sizes[taker]) // 2
    room = jnp.where((giver == sequence[0]) | (taker == sequence[0]) | (sizes[taker] == 0), 0, jnp.maximum(room, 0))
    passed = jax.random.randint(jax.random.fold_in(own, 4), (count // 2,), 0, 1 << 20) % (room + 1)
    sizes = sizes.at[giver].add(-passed).at[taker].add(passed)
    items = jnp.searchsorted(jnp.cumsum(sizes), jnp.arange(rows * top), side="right").astype(jnp.int32)
    listing = items.reshape(top, rows).T
    listing = listing[jax.random.permutation(jax.random.fold_in(own, 1), rows)]
    offset_by = jax.random.randint(jax.random.fold_in(own, 2), (rows, 1), 0, top)
    return jnp.take_along_axis(listing, (jnp.arange(top)[None, :] + offset_by) % top, axis=1)


def portions_of(number_of, total, bound, slope, full):
    weights = [(1 << 20) // math.isqrt(standing ** slope) + 1 for standing in range(1, number_of + 1)]
    largest = bound if full else min(bound, max(-(-total // number_of), total * weights[0] // sum(weights)))
    least = 1 if total - largest >= number_of - 1 else 0
    counts, rest = [largest] + [least] * (number_of - 1), total - largest - least * (number_of - 1)
    while rest > 0:
        candidates = [i for i in range(1, number_of) if counts[i] < largest] or [i for i in range(1, number_of) if counts[i] < bound]
        pool, remaining = sum([weights[i] for i in candidates]), rest
        for i in candidates:
            more = min(bound - counts[i], max(1, remaining * weights[i] // pool), rest)
            counts[i] = counts[i] + more
            rest = rest - more
    return np.array(counts)


def noise(own_key, extent, width, limit, cuts=(), held_as=jnp.bfloat16):
    factor_of = shard_levels(own_key, extent, cuts, -0.22, 0.18) if cuts else 1.0
    entries = jax.random.normal(own_key, extent, jnp.float32) * width * factor_of
    return jnp.minimum(jnp.maximum(entries, -limit), limit).astype(held_as)


def setup_inputs(seed: int = 0, part: int = 0) -> dict:
    key_list = jax.random.split(jax.random.key(seed), 8)
    own_keys = jax.random.split(jax.random.fold_in(key_list[7], part), 8)
    tokens = noise(own_keys[0], (TOKENS, D), 1.0, 6.0, ((0, 32),))
    expert_ids_keys = jax.random.split(jax.random.fold_in(own_keys[1], 1), TOKENS // TOK_DEV)
    expert_ids_turns = jax.random.permutation(jax.random.fold_in(own_keys[1], 3), TOKENS // TOK_DEV)
    expert_ids = jax.vmap(lambda own, number: shared_out(jax.random.fold_in(own_keys[1], 2), own, number, TOK_DEV, EXPERTS, TOP, CAP, 2))(expert_ids_keys, expert_ids_turns).reshape((TOKENS, TOP))
    gate_scores = jnp.clip(0.1 + 0.9 * jax.random.uniform(own_keys[2], (TOKENS, TOP), jnp.float32) ** shard_levels(own_keys[2], (TOKENS, TOP), ((0, 32),), -0.2, 0.2), 0.1, 1.0)
    gate_weight = noise(own_keys[3], (EXPERTS, D, F), D ** -0.5, 0.109375, ((0, 8), (1, 4)))
    up_weight = noise(own_keys[4], (EXPERTS, D, F), D ** -0.5, 0.109375, ((0, 8), (1, 4)))
    down_weight = noise(own_keys[5], (EXPERTS, D, F), F ** -0.5, 0.5, ((0, 8), (1, 4)))
    grad_out = noise(own_keys[6], (TOKENS, D), 1.0, 6.0, ((0, 32),))
    return {"tokens": tokens, "expert_ids": expert_ids, "gate_scores": gate_scores, "gate_weight": gate_weight, "up_weight": up_weight, "down_weight": down_weight, "grad_out": grad_out}


def group_partial(left, right):
    left_groups = left.astype(jnp.float32).reshape(-1, N_DP, TOK_DEV, left.shape[1])
    right_groups = right.astype(jnp.float32).reshape(-1, N_DP, TOK_DEV, right.shape[1])
    partial_sums = jnp.einsum("bgtd,bgtf->gdf", left_groups, right_groups)
    rounded = lax.optimization_barrier(partial_sums.astype(jnp.bfloat16))
    return jnp.sum(rounded.astype(jnp.float32), axis=0)


def reference(tokens, expert_ids, gate_scores, gate_weight, up_weight, down_weight, grad_out):
    total = tokens.shape[0]
    model_width = tokens.shape[1]
    grad_float = grad_out.astype(jnp.float32)

    def one_expert(carry, inputs):
        mixed_acc, input_acc, score_acc = carry
        expert_index, gate_mat, up_mat, down_mat = inputs
        gate_pre = jnp.dot(tokens, gate_mat, preferred_element_type=jnp.float32)
        up_pre = jnp.dot(tokens, up_mat, preferred_element_type=jnp.float32)
        sigmoid_gate = jax.nn.sigmoid(gate_pre)
        hidden_act = (gate_pre * sigmoid_gate * up_pre).astype(jnp.bfloat16)
        expert_out = jnp.dot(hidden_act, down_mat.T, preferred_element_type=jnp.float32).astype(jnp.bfloat16)
        chosen = expert_ids == expert_index
        weight_sel = jnp.sum(jnp.where(chosen, gate_scores, jnp.float32(0.0)), axis=1)
        out_float = expert_out.astype(jnp.float32)
        mixed_acc = mixed_acc + weight_sel[:, None] * out_float
        score_acc = score_acc + jnp.where(chosen, jnp.sum(grad_float * out_float, axis=1)[:, None], jnp.float32(0.0))
        grad_row = (weight_sel[:, None] * grad_float).astype(jnp.bfloat16)
        grad_act = jnp.dot(grad_row, down_mat, preferred_element_type=jnp.float32)
        gate_grad = (grad_act * up_pre * sigmoid_gate * (1.0 + gate_pre * (1.0 - sigmoid_gate))).astype(jnp.bfloat16)
        up_grad = (grad_act * gate_pre * sigmoid_gate).astype(jnp.bfloat16)
        input_grad = (jnp.dot(gate_grad, gate_mat.T, preferred_element_type=jnp.float32)
                      + jnp.dot(up_grad, up_mat.T, preferred_element_type=jnp.float32)).astype(jnp.bfloat16)
        input_acc = input_acc + input_grad.astype(jnp.float32)
        gate_term = group_partial(tokens, gate_grad)
        up_term = group_partial(tokens, up_grad)
        down_term = group_partial(grad_row, hidden_act)
        return (mixed_acc, input_acc, score_acc), (gate_term, up_term, down_term)

    start = (jnp.zeros((total, model_width), jnp.float32), jnp.zeros((total, model_width), jnp.float32),
             jnp.zeros((total, TOP), jnp.float32))
    indices = jnp.arange(EXPERTS, dtype=jnp.int32)
    (mixed_acc, input_acc, score_acc), (gate_grads, up_grads, down_grads) = lax.scan(
        one_expert, start, (indices, gate_weight, up_weight, down_weight))
    return (mixed_acc.astype(jnp.bfloat16), input_acc.astype(jnp.bfloat16), score_acc,
            gate_grads, up_grads, down_grads)
```

```python
import functools

import jax
import jax.numpy as jnp
from jax import lax
from jax.experimental import pallas as pl
from jax.experimental.pallas import tpu as pltpu
from jax.sharding import PartitionSpec as P

MESH = pl.DeviceIdType.MESH
F32 = jnp.float32
BF16 = jnp.bfloat16
NY = 4
NX = 4
N_COPIES = 96


def dot(a, b):
    return jnp.dot(a, b, preferred_element_type=F32)


def dot_t(a, b):
    return lax.dot_general(a, b, (((1,), (1,)), ((), ())), preferred_element_type=F32)


def kernel(
    tok, go, ids, scores, wg, wu, wd,
    lo, gt, gs, dg, du, dd,
    tokb, gob, sb, wb, tok_t, go_t, gub, hsb, gsb,
    dwb, dwr, zsend, zrecv, lop, gtp, lor, gtr, gsr,
    send, recv, local_sem,
):
    rows, width = tok.shape
    part = wg.shape[0]
    hidden = wg.shape[1]
    sec, ei, x = lax.axis_index("section"), lax.axis_index("expert"), lax.axis_index("dp")
    y, zh = ei // 2, ei % 2
    other = y * 2 + 1 - zh
    z_peer = (sec, other, x)

    def y_peer(d):
        return (sec, ((y + d) % NY) * 2 + zh, x)

    def x_peer(d):
        return (sec, ei, (x + d) % NX)

    peers = [z_peer] + [y_peer(d) for d in (1, 2, 3)] + [x_peer(d) for d in (1, 2, 3)]
    barrier = pltpu.get_barrier_semaphore()
    for p in peers:
        pl.semaphore_signal(barrier, inc=1, device_id=p, device_id_type=MESH)

    count = [0]

    def copy(src, dst, to):
        k = count[0]
        count[0] = k + 1
        return pltpu.make_async_remote_copy(
            src_ref=src, dst_ref=dst, send_sem=send.at[k], recv_sem=recv.at[k],
            device_id=to, device_id_type=MESH,
        )

    lane = lax.broadcasted_iota(jnp.int32, (rows, hidden), 1)

    def x_rows(d):
        return pl.ds(pl.multiple_of(((x + d) % NX) * part, part), part)

    def slot(j):
        return pl.ds(j * rows, rows)

    mine = x_rows(0)
    w_in = (wg, wu, wd)
    own = [pltpu.make_async_copy(tok, tokb.at[slot(0)], local_sem.at[0]),
           pltpu.make_async_copy(go, gob.at[slot(0)], local_sem.at[1])]
    own += [pltpu.make_async_copy(w_in[i], wb.at[0, i, mine], local_sem.at[2 + i]) for i in range(3)]
    for c in own:
        c.start()
    table = jnp.zeros((rows, hidden), F32)
    for k in range(ids.shape[1]):
        table += jnp.where(lane == ids[:, k : k + 1], scores[:, k : k + 1], 0.0)
    sb[0] = table

    pl.semaphore_wait(barrier, len(peers))

    z_w = [copy(w_in[i], wb.at[1, i, mine], z_peer) for i in range(3)]
    y_s = [copy(sb.at[0], sb.at[NY - d], y_peer(d)) for d in (2, 1, 3)]
    y_tok = [copy(tok, tokb.at[slot(NY - d)], y_peer(d)) for d in (2, 1, 3)]
    y_go = [copy(go, gob.at[slot(NY - d)], y_peer(d)) for d in (2, 1, 3)]
    x_w = [copy(w_in[i], wb.at[0, i, mine], x_peer(d)) for i in range(3) for d in (2, 1, 3)]
    for c in z_w + y_s + x_w + y_tok + y_go:
        c.start()

    x_r = []
    for i in range(3):
        z_w[i].wait_recv()
        for d in (2, 1, 3):
            c = copy(wb.at[1, i, mine], wb.at[1, i, mine], x_peer(d))
            c.start()
            x_r.append(c)

    for c in own:
        c.wait()
    for c in y_s + y_tok + y_go:
        c.wait_recv()

    def flip(j, _):
        r = pl.ds(pl.multiple_of(j * rows, rows), rows)
        for s in range(NX):
            cols = pl.ds(s * part, part)
            tok_t[cols, r] = tokb[r, cols].T
            go_t[cols, r] = gob[r, cols].T
        return 0

    for j in range(NY):
        flip(j, 0)

    block = 2 * rows

    def hidden_rows(r, e):
        def step(m, _):
            at = pl.ds(pl.multiple_of(m * block, block), block)
            pre = jnp.zeros((block, 2 * hidden), F32)
            act = jnp.zeros((block, hidden), F32)
            for s in range(NX):
                cols = pl.ds(s * part, part)
                pre += dot(tokb[at, cols], jnp.concatenate([wb[r, 0, cols], wb[r, 1, cols]], axis=1))
                act += dot(gob[at, cols], wb[r, 2, cols])
            g, u = pre[:, :hidden], pre[:, hidden:]
            sc = jnp.concatenate([sb[2 * m], sb[2 * m + 1]], axis=0)
            big = lax.broadcasted_iota(jnp.int32, (block, hidden), 1)
            sc = jnp.sum(jnp.where(big == e, sc, 0.0), axis=1, keepdims=True)
            sig = jax.nn.sigmoid(g)
            silu = g * sig
            h = silu * u
            ga = sc * act
            hsb[r, at] = (sc * h).astype(BF16)
            gub[r, at, :hidden] = (ga * u * sig * (1.0 + g * (1.0 - sig))).astype(BF16)
            gub[r, at, hidden:] = (ga * silu).astype(BF16)
            score = jnp.sum(h * act, axis=1, keepdims=True)
            score = jnp.where(big == e, score, 0.0)
            for n in range(2):
                piece = score[n * rows : (n + 1) * rows]
                if r == 1:
                    gsb[2 * m + n] = piece
                else:
                    gsb[2 * m + n] += piece
            return 0

        lax.fori_loop(0, NY // 2, step, 0)

    def weight_grads(r, d):
        at = x_rows(d)
        both = dot(tok_t[at], gub[r]).astype(BF16)
        dwb[r, 0, at] = both[:, :hidden]
        dwb[r, 1, at] = both[:, hidden:]
        dwb[r, 2, at] = dot(go_t[at], hsb[r]).astype(BF16)
        if d == 0:
            return []
        cs = []
        for i in range(3):
            c = copy(dwb.at[r, i, at], dwr.at[r, NX - d - 1, i], x_peer(d))
            c.start()
            cs.append(c)
        return cs

    def outputs(j):
        at = slot(j)
        h = jnp.concatenate([hsb[0, at], hsb[1, at]], axis=1)
        g0, g1 = gub[0, at], gub[1, at]

        def step(s, _):
            cols = pl.ds(pl.multiple_of(s * part, part), part)
            down = jnp.concatenate([wb[0, 2, cols], wb[1, 2, cols]], axis=1)
            lop[at, cols] = dot_t(h, down).astype(BF16)
            back = dot_t(g0, jnp.concatenate([wb[0, 0, cols], wb[0, 1, cols]], axis=1))
            back += dot_t(g1, jnp.concatenate([wb[1, 0, cols], wb[1, 1, cols]], axis=1))
            gtp[at, cols] = back.astype(BF16)
            return 0

        lax.fori_loop(0, NX, step, 0)
        if j == 0:
            return []
        cs = [copy(gsb.at[j], gsr.at[NY - j - 1], y_peer(j)),
              copy(lop.at[at], lor.at[NY - j - 1], y_peer(j)),
              copy(gtp.at[at], gtr.at[NY - j - 1], y_peer(j))]
        for c in cs:
            c.start()
        return cs

    def summed(r, i):
        total = dwb[r, i, mine].astype(F32)
        for n in range(NX - 1):
            total += dwr[r, n, i].astype(F32)
        return total

    for c in x_r:
        c.wait_recv()
    hidden_rows(1, other)
    x_d1 = []
    for d in (2, 1, 3, 0):
        x_d1 += weight_grads(1, d)
    for c in x_w:
        c.wait_recv()
    hidden_rows(0, ei)
    z_d = []
    y_o = []
    for i, j in enumerate((2, 1, 3)):
        for c in x_d1[i::3]:
            c.wait_recv()
        zsend[i] = summed(1, i).astype(BF16)
        c = copy(zsend.at[i], zrecv.at[i], z_peer)
        c.start()
        z_d.append(c)
        y_o += outputs(j)
    x_d0 = []
    for d in (2, 1, 3, 0):
        x_d0 += weight_grads(0, d)
    outputs(0)

    for c in x_d0:
        c.wait_recv()
    for c in y_o:
        c.wait_recv()
    lo_sum, gt_sum, gs_sum = lop[slot(0)].astype(F32), gtp[slot(0)].astype(F32), gsb[0]
    for n in range(NY - 1):
        lo_sum += lor[n].astype(F32)
        gt_sum += gtr[n].astype(F32)
        gs_sum += gsr[n]
    lo[...] = lo_sum.astype(BF16)
    gt[...] = gt_sum.astype(BF16)
    for k in range(ids.shape[1]):
        gs[:, k : k + 1] = jnp.sum(jnp.where(lane == ids[:, k : k + 1], gs_sum, 0.0), axis=1, keepdims=True)
    for i, out in enumerate((dg, du, dd)):
        z_d[i].wait_recv()
        out[...] = summed(0, i) + zrecv[i].astype(F32)
    for c in z_w + y_s + y_tok + y_go + x_w + x_r + x_d1 + z_d + y_o + x_d0:
        c.wait_send()


def local(tokens, expert_ids, gate_scores, gate_weight, up_weight, down_weight, grad_out):
    rows, width = tokens.shape
    _, part, hidden = gate_weight.shape
    top = expert_ids.shape[1]
    vmem, hbm = pl.BlockSpec(memory_space=pltpu.VMEM), pl.BlockSpec(memory_space=pl.ANY)
    shape = jax.ShapeDtypeStruct
    scratch = [
        pltpu.VMEM((NY * rows, width), BF16),
        pltpu.VMEM((NY * rows, width), BF16),
        pltpu.VMEM((NY, rows, hidden), F32),
        pltpu.VMEM((2, 3, width, hidden), BF16),
        pltpu.VMEM((width, NY * rows), BF16),
        pltpu.VMEM((width, NY * rows), BF16),
        pltpu.VMEM((2, NY * rows, 2 * hidden), BF16),
        pltpu.VMEM((2, NY * rows, hidden), BF16),
        pltpu.VMEM((NY, rows, hidden), F32),
        pltpu.VMEM((2, 3, width, hidden), BF16),
        pltpu.VMEM((2, NX - 1, 3, part, hidden), BF16),
        pltpu.VMEM((3, part, hidden), BF16),
        pltpu.VMEM((3, part, hidden), BF16),
        pltpu.VMEM((NY * rows, width), BF16),
        pltpu.VMEM((NY * rows, width), BF16),
        pltpu.VMEM((NY - 1, rows, width), BF16),
        pltpu.VMEM((NY - 1, rows, width), BF16),
        pltpu.VMEM((NY - 1, rows, hidden), F32),
        pltpu.SemaphoreType.DMA((N_COPIES,)),
        pltpu.SemaphoreType.DMA((N_COPIES,)),
        pltpu.SemaphoreType.DMA((5,)),
    ]
    lo, gt, gs, dg, du, dd = pl.pallas_call(
        kernel,
        out_shape=[
            shape((rows, width), BF16),
            shape((rows, width), BF16),
            shape((rows, top), F32),
            shape((part, hidden), F32),
            shape((part, hidden), F32),
            shape((part, hidden), F32),
        ],
        in_specs=[hbm, hbm, vmem, vmem, hbm, hbm, hbm],
        out_specs=[vmem] * 6,
        scratch_shapes=scratch,
        compiler_params=pltpu.CompilerParams(
            collective_id=0, has_side_effects=True, vmem_limit_bytes=60 << 20
        ),
    )(tokens, grad_out, expert_ids, gate_scores, gate_weight[0], up_weight[0], down_weight[0])
    return lo, gt, gs, dg[None], du[None], dd[None]


def solution(mesh):
    rows_p = P(("section", "expert", "dp"), None)
    weight_p = P(("section", "expert"), "dp", None)
    return jax.shard_map(
        local,
        mesh=mesh,
        in_specs=(rows_p, rows_p, rows_p, weight_p, weight_p, weight_p, rows_p),
        out_specs=(rows_p, rows_p, rows_p, weight_p, weight_p, weight_p),
        check_vma=False,
    )
```

```python
import jax
import jax.numpy as jnp
from jax import lax
from jax.experimental import pallas as pl
from jax.experimental.pallas import tpu as pltpu
from jax.sharding import PartitionSpec as P

MESH = pl.DeviceIdType.MESH
F32 = jnp.float32
BF16 = jnp.bfloat16
NY = 4
NX = 4
N_COPIES = 128


def dot(a, b):
    return jnp.dot(a, b, preferred_element_type=F32)


def dot_t(a, b):
    return lax.dot_general(a, b, (((1,), (1,)), ((), ())), preferred_element_type=F32)


def dot_l(a, b):
    return lax.dot_general(a, b, (((0,), (0,)), ((), ())), preferred_element_type=F32)


def swap(a):
    return pltpu.roll(a.astype(F32), a.shape[1] // 2, axis=1)


def low(shape):
    return lax.broadcasted_iota(jnp.int32, shape, 1) < shape[1] // 2


def kernel(
    tok, go, ids, scores, wg, wu, wd,
    lo, gt, gs, dg, du, dd,
    tokb, gob, tab, sbc, wb, pk, rw, rd, rdn,
    pre, act, act2, gub, hsb, hdup, guh, gst, gsr,
    dwb, dwr, dwq, dwqr, zsend, zrecv, lop, gtp, far, lor, gtr, dout,
    send, recv, local_sem, out_sem,
):
    rows, width = tok.shape
    part, hidden = wg.shape
    half, hp = rows // 2, part // 2
    sec, ei, x = lax.axis_index("section"), lax.axis_index("expert"), lax.axis_index("dp")
    y, zh = ei // 2, ei % 2
    other = y * 2 + 1 - zh
    z_peer = (sec, other, x)

    def y_peer(d):
        return (sec, ((y + d) % NY) * 2 + zh, x)

    def x_peer(d):
        return (sec, ei, (x + d) % NX)

    peers = [z_peer] + [y_peer(d) for d in (1, 2, 3)] + [x_peer(d) for d in (1, 2, 3)]
    barrier = pltpu.get_barrier_semaphore()
    for p in peers:
        pl.semaphore_signal(barrier, inc=1, device_id=p, device_id_type=MESH)

    made = []

    def copy(src, dst, to):
        k = len(made)
        c = pltpu.make_async_remote_copy(
            src_ref=src, dst_ref=dst, send_sem=send.at[k], recv_sem=recv.at[k],
            device_id=to, device_id_type=MESH,
        )
        made.append(c)
        c.start()
        return c

    def x_rows(d, size):
        return pl.ds(pl.multiple_of(((x + d) % NX) * size, size), size)

    def slot(j):
        return pl.ds(j * rows, rows)

    mine, mine_d = x_rows(0, part), x_rows(0, hp)
    w_in = (wg, wu, wd)
    own_w = [pltpu.make_async_copy(w_in[i], wb.at[i, mine], local_sem.at[i]) for i in range(3)]
    own_t = [pltpu.make_async_copy(tok, tokb.at[slot(0)], local_sem.at[3]),
             pltpu.make_async_copy(go, gob.at[slot(0)], local_sem.at[4])]
    for c in own_w + own_t:
        c.start()

    sub = lax.broadcasted_iota(jnp.int32, tab.shape[1:], 0)
    table = jnp.zeros(sub.shape, F32)
    for k in range(ids.shape[0]):
        table += jnp.where(sub == ids[k : k + 1], scores[k : k + 1], 0.0)
    tab[0] = table

    for c in own_w:
        c.wait()
    g, u, d = wb[0, mine].astype(F32), wb[1, mine].astype(F32), wb[2, mine].astype(F32)
    lw, ld = low((part, hidden)), low((hp, hidden))
    for h in range(2):
        if h == 0:
            gu = jnp.where(lw, g, swap(u)).astype(BF16)
            dn = jnp.where(ld, d[:hp], swap(d[hp:])).astype(BF16)
        else:
            gu = jnp.where(lw, swap(g), u).astype(BF16)
            dn = jnp.where(ld, swap(d[:hp]), d[hp:]).astype(BF16)
        pk[h, 0], pk[h, 1], pk[h, 2] = gu[:hp], gu[hp:], dn

    pl.semaphore_wait(barrier, len(peers))

    def unit(h, c):
        if c == 2:
            return rd.at[h, mine_d]
        return rw.at[h, pl.ds(pl.multiple_of(x * part + c * hp, hp), hp)]

    units = [(h, c) for h in range(2) for c in range(3)]
    z_w = [copy(pk.at[h, c], unit(h, c), z_peer) for h, c in units]
    y_s = [copy(tab.at[0], tab.at[NY - d], y_peer(d)) for d in (2, 1, 3)]
    bufs = ((tok, tokb), (go, gob))
    y_a, y_b = [], []
    for first in (True, False):
        for src, dst in bufs:
            for d in (1, 3):
                r0 = 0 if (d == 1) == first else half
                c = copy(src.at[pl.ds(r0, half)], dst.at[pl.ds((NY - d) * rows + r0, half)], y_peer(d))
                (y_a if first else y_b).append(c)
    x_w = [copy(w_in[i], wb.at[i, mine], x_peer(d)) for i in range(3) for d in (2, 1, 3)]

    y_c = []
    for n, (_, dst) in enumerate(bufs):
        for m, d in enumerate((1, 3)):
            y_a[2 * n + m].wait_recv()
            r0 = 0 if d == 1 else half
            c = copy(dst.at[pl.ds((NY - d) * rows + r0, half)], dst.at[pl.ds(2 * rows + r0, half)], y_peer(d))
            y_c.append(c)

    x_r = [[], []]

    def pass_on(n):
        h, c = units[n]
        z_w[n].wait_recv()
        for d in (2, 1, 3):
            x_r[h].append(copy(unit(h, c), unit(h, c), x_peer(d)))

    pass_on(0)
    for c in y_s:
        c.wait_recv()
    for r, e in ((0, ei), (1, other)):
        for j in range(NY):
            row = jnp.sum(jnp.where(sub == e, tab[j], 0.0), axis=0, keepdims=True)
            sbc[r, slot(j)] = jnp.broadcast_to(row, (rows, hidden)).T
    for n in (1, 2, 3):
        pass_on(n)
    for c in own_t:
        c.wait()
    for c in y_b + y_c:
        c.wait_recv()

    def add_score(j, e, col):
        flat = jnp.broadcast_to(col, (rows, hidden)).T[: sub.shape[0]]
        gst[j] += jnp.where(sub == e, flat, 0.0)

    for j in range(NY):
        gst[j] = jnp.zeros(sub.shape, F32)

    def hidden_own():
        pre[...] = dot(tokb[...], jnp.concatenate([wb[0], wb[1]], axis=1))
        act[...] = dot(gob[...], wb[2])

        def step(j, _):
            at = pl.ds(pl.multiple_of(j * rows, rows), rows)
            g, u, a, s = pre[at, :hidden], pre[at, hidden:], act[at], sbc[0, at]
            sig = jax.nn.sigmoid(g)
            silu = g * sig
            h = silu * u
            ga = s * a
            hsb[0, at] = (s * h).astype(BF16)
            gub[0, at, :hidden] = (ga * u * sig * (1.0 + g * (1.0 - sig))).astype(BF16)
            gub[0, at, hidden:] = (ga * silu).astype(BF16)
            add_score(j, ei, jnp.sum(h * a, axis=1, keepdims=True))
            return 0

        lax.fori_loop(0, NY, step, 0)

    lr = low((rows, hidden))

    def hidden_other(h):
        pre[:, :hidden] = dot(tokb[...], rw[h])
        for s in range(NX):
            dn = rd[h, pl.ds(s * hp, hp)]
            a1 = dot(gob[:, pl.ds(s * part, hp)], dn)
            a2 = dot(gob[:, pl.ds(s * part + hp, hp)], dn)
            if s == 0:
                act[...], act2[...] = a1, a2
            else:
                act[...] += a1
                act2[...] += a2

        def step(j, _):
            at = pl.ds(pl.multiple_of(j * rows, rows), rows)
            p, s = pre[at, :hidden], sbc[1, at]
            q = swap(p)
            g, u = jnp.where(lr, p, q), jnp.where(lr, q, p)
            a = act[at] + swap(act2[at])
            a = jnp.where(lr, a, swap(a))
            sig = jax.nn.sigmoid(g)
            silu = g * sig
            hid = silu * u
            ga = s * a
            hs = (s * hid).astype(BF16)
            hdup[h, at] = hs
            gu = jnp.where(lr, ga * u * sig * (1.0 + g * (1.0 - sig)), ga * silu)
            guh[h, at] = gu.astype(BF16)
            gub[1, at, h * hidden : (h + 1) * hidden] = gu.astype(BF16)
            add_score(j, other, jnp.sum(jnp.where(lr, hid * a, 0.0), axis=1, keepdims=True))
            return 0

        lax.fori_loop(0, NY, step, 0)

    def grads_other(h):
        cs = [[], [], []]
        for d in (2, 1, 3, 0):
            at = x_rows(d, part)
            gu = dot_l(tokb[:, at], guh[h]).astype(BF16)
            dn = dot_l(gob[:, at], hdup[h])
            dwq[h, d, 0], dwq[h, d, 1] = gu[:hp], gu[hp:]
            dwq[h, d, 2] = jnp.where(ld, dn[:hp], dn[hp:]).astype(BF16)
            if d:
                for c in range(3):
                    cs[c].append(copy(dwq.at[h, d, c], dwqr.at[h, NX - d - 1, c], x_peer(d)))
        return cs

    def send_z(h, c, arrivals):
        for a in arrivals:
            a.wait_recv()
        total = dwq[h, 0, c].astype(F32)
        for n in range(NX - 1):
            total += dwqr[h, n, c].astype(F32)
        zsend[h, c] = total.astype(BF16)
        return copy(zsend.at[h, c], zrecv.at[h, c], z_peer)

    for c in x_r[0]:
        c.wait_recv()
    hidden_other(0)
    x_d1 = [grads_other(0), None]
    pass_on(4)
    for c in x_w:
        c.wait_recv()
    hidden_own()
    z_d = [send_z(0, 0, x_d1[0][0])]
    pass_on(5)
    for c in (1, 2):
        z_d.append(send_z(0, c, x_d1[0][c]))

    for c in x_r[1]:
        c.wait_recv()
    hidden_other(1)
    lall = low((hp, hidden))
    for s in range(NX):
        d0, d1 = rd[0, pl.ds(s * hp, hp)].astype(F32), rd[1, pl.ds(s * hp, hp)].astype(F32)
        rdn[pl.ds(s * part, hp)] = jnp.where(lall, d0, swap(d1)).astype(BF16)
        rdn[pl.ds(s * part + hp, hp)] = jnp.where(lall, swap(d0), d1).astype(BF16)
    lfull = low((NY * rows, hidden))
    hsb[1] = jnp.where(lfull, hdup[0].astype(F32), hdup[1].astype(F32)).astype(BF16)

    hs = jnp.concatenate([hsb[0], hsb[1]], axis=1)
    gu = jnp.concatenate([gub[0], gub[1]], axis=1)
    y_far = []
    for s in range(NX):
        cols = pl.ds(s * part, part)
        lop[:, cols] = dot_t(hs, jnp.concatenate([wb[2, cols], rdn[cols]], axis=1)).astype(BF16)
        both = jnp.concatenate([wb[0, cols], wb[1, cols], rw[0, cols], rw[1, cols]], axis=1)
        gtp[:, cols] = dot_t(gu, both).astype(BF16)
        for n, buf in enumerate((lop, gtp)):
            for m, d in enumerate((1, 3)):
                r0 = m * half
                c = copy(buf.at[pl.ds(2 * rows + r0, half), cols], far.at[n, m, :, cols], y_peer(d))
                y_far.append(c)
    y_g = [copy(gst.at[d], gsr.at[NY - d - 1], y_peer(d)) for d in (2, 1, 3)]
    y_o = []
    for buf, dst in ((lop, lor), (gtp, gtr)):
        for m, d in enumerate((1, 3)):
            r0 = half - m * half
            y_o.append(copy(buf.at[pl.ds(d * rows + r0, half)], dst.at[m, pl.ds(r0, half)], y_peer(d)))
    x_d1[1] = grads_other(1)
    k = 0
    for s in range(NX):
        cols = pl.ds(s * part, part)
        for n, (buf, dst) in enumerate(((lop, lor), (gtp, gtr))):
            for m, d in enumerate((1, 3)):
                r0 = m * half
                y_far[k].wait_recv()
                k += 1
                at = pl.ds(d * rows + r0, half)
                buf[at, cols] = (buf[at, cols].astype(F32) + far[n, m, :, cols].astype(F32)).astype(BF16)
                y_o.append(copy(buf.at[at, cols], dst.at[m, pl.ds(r0, half), cols], y_peer(d)))
        if s < 3:
            z_d.append(send_z(1, s, x_d1[1][s]))

    x_d0 = []
    for d in (2, 1, 3, 0):
        at = x_rows(d, part)
        both = dot_l(tokb[:, at], gub[0]).astype(BF16)
        dwb[d, 0], dwb[d, 1] = both[:, :hidden], both[:, hidden:]
        dwb[d, 2] = dot_l(gob[:, at], hsb[0]).astype(BF16)
        if d:
            for i in range(3):
                x_d0.append(copy(dwb.at[d, i], dwr.at[NX - d - 1, i], x_peer(d)))
    for c in x_d0:
        c.wait_recv()
    for i in range(3):
        total = dwb[0, i].astype(F32)
        for n in range(NX - 1):
            total += dwr[n, i].astype(F32)
        dout[i] = total

    outs = []
    for c in y_g + y_o:
        c.wait_recv()
    for n, (buf, got, out) in enumerate(((lop, lor, lo), (gtp, gtr, gt))):
        total = buf[slot(0)].astype(F32) + got[0].astype(F32) + got[1].astype(F32)
        buf[slot(0)] = total.astype(BF16)
        c = pltpu.make_async_copy(buf.at[slot(0)], out, out_sem.at[n])
        c.start()
        outs.append(c)
    gs_sum = gst[0] + gsr[0] + gsr[1] + gsr[2]
    for k in range(ids.shape[0]):
        gs[k : k + 1] = jnp.sum(jnp.where(sub == ids[k : k + 1], gs_sum, 0.0), axis=0, keepdims=True)

    for c in z_d:
        c.wait_recv()
    for c in range(2):
        at = pl.ds(c * hp, hp)
        p1, p2 = zrecv[0, c].astype(F32), zrecv[1, c].astype(F32)
        dout[0, at] += jnp.where(ld, p1, swap(p2))
        dout[1, at] += jnp.where(ld, swap(p1), p2)
    q1, q2 = zrecv[0, 2].astype(F32), zrecv[1, 2].astype(F32)
    dout[2, pl.ds(0, hp)] += jnp.where(ld, q1, swap(q2))
    dout[2, pl.ds(hp, hp)] += jnp.where(ld, swap(q1), q2)
    for i, out in enumerate((dg, du, dd)):
        c = pltpu.make_async_copy(dout.at[i], out, out_sem.at[2 + i])
        c.start()
        outs.append(c)
    for c in made:
        c.wait_send()
    for c in outs:
        c.wait()


def hand_on(*refs):
    n = (len(refs) - 1) // 2
    cs = [pltpu.make_async_copy(refs[i], refs[n + i], refs[-1].at[i]) for i in range(n)]
    for c in cs:
        c.start()
    for c in cs:
        c.wait()


def local(tokens, expert_ids, gate_scores, gate_weight, up_weight, down_weight, grad_out):
    rows, width = tokens.shape
    _, part, hidden = gate_weight.shape
    top = expert_ids.shape[1]
    experts = lax.axis_size("expert")
    all_rows, half, hp = NY * rows, rows // 2, part // 2
    vmem, hbm = pl.BlockSpec(memory_space=pltpu.VMEM), pl.BlockSpec(memory_space=pl.ANY)
    shape = jax.ShapeDtypeStruct
    v = pltpu.VMEM
    scratch = [
        v((all_rows, width), BF16),
        v((all_rows, width), BF16),
        v((NY, experts, rows), F32),
        v((2, all_rows, hidden), F32),
        v((3, width, hidden), BF16),
        v((2, 3, hp, hidden), BF16),
        v((2, width, hidden), BF16),
        v((2, width // 2, hidden), BF16),
        v((width, hidden), BF16),
        v((all_rows, 2 * hidden), F32),
        v((all_rows, hidden), F32),
        v((all_rows, hidden), F32),
        v((2, all_rows, 2 * hidden), BF16),
        v((2, all_rows, hidden), BF16),
        v((2, all_rows, hidden), BF16),
        v((2, all_rows, hidden), BF16),
        v((NY, experts, rows), F32),
        v((NY - 1, experts, rows), F32),
        v((NX, 3, part, hidden), BF16),
        v((NX - 1, 3, part, hidden), BF16),
        v((2, NX, 3, hp, hidden), BF16),
        v((2, NX - 1, 3, hp, hidden), BF16),
        v((2, 3, hp, hidden), BF16),
        v((2, 3, hp, hidden), BF16),
        v((all_rows, width), BF16),
        v((all_rows, width), BF16),
        v((2, 2, half, width), BF16),
        v((2, rows, width), BF16),
        v((2, rows, width), BF16),
        v((3, part, hidden), F32),
        pltpu.SemaphoreType.DMA((N_COPIES,)),
        pltpu.SemaphoreType.DMA((N_COPIES,)),
        pltpu.SemaphoreType.DMA((5,)),
        pltpu.SemaphoreType.DMA((5,)),
    ]
    big, weight = shape((rows, width), BF16), shape((part, hidden), F32)
    shapes = [big, big, shape((top, rows), F32), weight, weight, weight]
    outs = pl.pallas_call(
        kernel,
        out_shape=shapes,
        in_specs=[hbm, hbm, vmem, vmem, hbm, hbm, hbm],
        out_specs=[hbm, hbm, vmem, hbm, hbm, hbm],
        scratch_shapes=scratch,
        compiler_params=pltpu.CompilerParams(
            collective_id=0, has_side_effects=True, vmem_limit_bytes=60 << 20
        ),
    )(tokens, grad_out, expert_ids.T, gate_scores.T, gate_weight[0], up_weight[0], down_weight[0])
    lo, gt, gs, dg, du, dd = pl.pallas_call(
        hand_on,
        out_shape=shapes,
        in_specs=[hbm] * 6,
        out_specs=[hbm] * 6,
        scratch_shapes=[pltpu.SemaphoreType.DMA((6,))],
    )(*outs)
    return lo, gt, gs.T, dg[None], du[None], dd[None]


def solution(mesh):
    rows_p = P(("section", "expert", "dp"), None)
    weight_p = P(("section", "expert"), "dp", None)
    return jax.shard_map(
        local,
        mesh=mesh,
        in_specs=(rows_p, rows_p, rows_p, weight_p, weight_p, weight_p, rows_p),
        out_specs=(rows_p, rows_p, rows_p, weight_p, weight_p, weight_p),
        check_vma=False,
    )
```

```python
import jax
import jax.numpy as jnp
from jax import lax
from jax.experimental import pallas as pl
from jax.experimental.pallas import tpu as pltpu
from jax.sharding import PartitionSpec as P

MESH = pl.DeviceIdType.MESH
F32 = jnp.float32
BF16 = jnp.bfloat16
NY = 4
NX = 4
N_COPIES = 128


def dot(a, b):
    return jnp.dot(a, b, preferred_element_type=F32)


def dot_t(a, b):
    return lax.dot_general(a, b, (((1,), (1,)), ((), ())), preferred_element_type=F32)


def dot_l(a, b):
    return lax.dot_general(a, b, (((0,), (0,)), ((), ())), preferred_element_type=F32)


def swap(a):
    return pltpu.roll(a.astype(F32), a.shape[1] // 2, axis=1)


def low(shape):
    return lax.broadcasted_iota(jnp.int32, shape, 1) < shape[1] // 2


def kernel(
    tok, go, ids, scores, wg, wu, wd,
    lo, gt, gs, dg, du, dd,
    tokb, gob, tab, sbc, wb, pk, rw, rd, rdn,
    pre, act, act2, gub, hsb, hdup, guh, gst, gsr,
    dwb, dwr, dwq, dwqr, zsend, zrecv, lop, gtp, far, lor, gtr, dout,
    send, recv, local_sem, out_sem,
):
    rows, width = tok.shape
    part, hidden = wg.shape
    half, hp = rows // 2, part // 2
    sec, ei, x = lax.axis_index("section"), lax.axis_index("expert"), lax.axis_index("dp")
    y, zh = ei // 2, ei % 2
    other = y * 2 + 1 - zh
    z_peer = (sec, other, x)

    def y_peer(d):
        return (sec, ((y + d) % NY) * 2 + zh, x)

    def x_peer(d):
        return (sec, ei, (x + d) % NX)

    peers = [z_peer] + [y_peer(d) for d in (1, 2, 3)] + [x_peer(d) for d in (1, 2, 3)]
    barrier = pltpu.get_barrier_semaphore()
    for p in peers:
        pl.semaphore_signal(barrier, inc=1, device_id=p, device_id_type=MESH)

    made = []

    def copy(src, dst, to):
        k = len(made)
        c = pltpu.make_async_remote_copy(
            src_ref=src, dst_ref=dst, send_sem=send.at[k], recv_sem=recv.at[k],
            device_id=to, device_id_type=MESH,
        )
        made.append(c)
        c.start()
        return c

    def x_rows(d, size):
        return pl.ds(pl.multiple_of(((x + d) % NX) * size, size), size)

    def slot(j):
        return pl.ds(j * rows, rows)

    mine, mine_d = x_rows(0, part), x_rows(0, hp)
    w_in = (wg, wu, wd)
    own_w = [pltpu.make_async_copy(w_in[i], wb.at[i, mine], local_sem.at[i]) for i in range(3)]
    own_t = [pltpu.make_async_copy(tok, tokb.at[slot(0)], local_sem.at[3]),
             pltpu.make_async_copy(go, gob.at[slot(0)], local_sem.at[4])]
    for c in own_w + own_t:
        c.start()

    sub = lax.broadcasted_iota(jnp.int32, tab.shape[1:], 0)
    table = jnp.zeros(sub.shape, F32)
    for k in range(ids.shape[0]):
        table += jnp.where(sub == ids[k : k + 1], scores[k : k + 1], 0.0)
    tab[0] = table

    for c in own_w:
        c.wait()
    g, u, d = wb[0, mine].astype(F32), wb[1, mine].astype(F32), wb[2, mine].astype(F32)
    lw, ld = low((part, hidden)), low((hp, hidden))
    for h in range(2):
        if h == 0:
            gu = jnp.where(lw, g, swap(u)).astype(BF16)
            dn = jnp.where(ld, d[:hp], swap(d[hp:])).astype(BF16)
        else:
            gu = jnp.where(lw, swap(g), u).astype(BF16)
            dn = jnp.where(ld, swap(d[:hp]), d[hp:]).astype(BF16)
        pk[h, 0], pk[h, 1], pk[h, 2] = gu[:hp], gu[hp:], dn

    pl.semaphore_wait(barrier, len(peers))

    def unit(h, c):
        if c == 2:
            return rd.at[h, mine_d]
        return rw.at[h, pl.ds(pl.multiple_of(x * part + c * hp, hp), hp)]

    units = [(h, c) for h in range(2) for c in range(3)]
    z_w = [copy(pk.at[h, c], unit(h, c), z_peer) for h, c in units]
    y_s = [copy(tab.at[0], tab.at[NY - d], y_peer(d)) for d in (2, 1, 3)]
    bufs = ((tok, tokb), (go, gob))
    y_a, y_b = [], []
    for first in (True, False):
        for src, dst in bufs:
            for d in (1, 3):
                r0 = 0 if (d == 1) == first else half
                c = copy(src.at[pl.ds(r0, half)], dst.at[pl.ds((NY - d) * rows + r0, half)], y_peer(d))
                (y_a if first else y_b).append(c)
    x_w = [copy(w_in[i], wb.at[i, mine], x_peer(d)) for i in range(3) for d in (2, 1, 3)]

    y_c = []
    for n, (_, dst) in enumerate(bufs):
        for m, d in enumerate((1, 3)):
            y_a[2 * n + m].wait_recv()
            r0 = 0 if d == 1 else half
            c = copy(dst.at[pl.ds((NY - d) * rows + r0, half)], dst.at[pl.ds(2 * rows + r0, half)], y_peer(d))
            y_c.append(c)

    x_r = [[], []]

    def pass_on(n):
        h, c = units[n]
        z_w[n].wait_recv()
        for d in (2, 1, 3):
            x_r[h].append(copy(unit(h, c), unit(h, c), x_peer(d)))

    pass_on(0)
    for c in y_s:
        c.wait_recv()
    for r, e in ((0, ei), (1, other)):
        for j in range(NY):
            row = jnp.sum(jnp.where(sub == e, tab[j], 0.0), axis=0, keepdims=True)
            sbc[r, slot(j)] = jnp.broadcast_to(row, (rows, hidden)).T
    for n in (1, 2, 3):
        pass_on(n)
    for c in own_t:
        c.wait()
    for c in y_b + y_c:
        c.wait_recv()

    def add_score(j, e, col):
        flat = jnp.broadcast_to(col, (rows, hidden)).T[: sub.shape[0]]
        gst[j] += jnp.where(sub == e, flat, 0.0)

    for j in range(NY):
        gst[j] = jnp.zeros(sub.shape, F32)

    def hidden_own():
        pre[...] = dot(tokb[...], jnp.concatenate([wb[0], wb[1]], axis=1))
        act[...] = dot(gob[...], wb[2])

        def step(j, _):
            at = pl.ds(pl.multiple_of(j * rows, rows), rows)
            g, u, a, s = pre[at, :hidden], pre[at, hidden:], act[at], sbc[0, at]
            sig = jax.nn.sigmoid(g)
            silu = g * sig
            h = silu * u
            ga = s * a
            hsb[0, at] = (s * h).astype(BF16)
            gub[0, at, :hidden] = (ga * u * sig * (1.0 + g * (1.0 - sig))).astype(BF16)
            gub[0, at, hidden:] = (ga * silu).astype(BF16)
            add_score(j, ei, jnp.sum(h * a, axis=1, keepdims=True))
            return 0

        lax.fori_loop(0, NY, step, 0)

    lr = low((rows, hidden))

    def hidden_other(h):
        pre[:, :hidden] = dot(tokb[...], rw[h])
        for s in range(NX):
            dn = rd[h, pl.ds(s * hp, hp)]
            a1 = dot(gob[:, pl.ds(s * part, hp)], dn)
            a2 = dot(gob[:, pl.ds(s * part + hp, hp)], dn)
            if s == 0:
                act[...], act2[...] = a1, a2
            else:
                act[...] += a1
                act2[...] += a2

        def step(j, _):
            at = pl.ds(pl.multiple_of(j * rows, rows), rows)
            p, s = pre[at, :hidden], sbc[1, at]
            q = swap(p)
            g, u = jnp.where(lr, p, q), jnp.where(lr, q, p)
            a = act[at] + swap(act2[at])
            a = jnp.where(lr, a, swap(a))
            sig = jax.nn.sigmoid(g)
            silu = g * sig
            hid = silu * u
            ga = s * a
            hs = (s * hid).astype(BF16)
            hdup[h, at] = hs
            gu = jnp.where(lr, ga * u * sig * (1.0 + g * (1.0 - sig)), ga * silu)
            guh[h, at] = gu.astype(BF16)
            gub[1, at, h * hidden : (h + 1) * hidden] = gu.astype(BF16)
            add_score(j, other, jnp.sum(jnp.where(lr, hid * a, 0.0), axis=1, keepdims=True))
            return 0

        lax.fori_loop(0, NY, step, 0)

    def grads_other(h):
        cs = [[], [], []]
        for d in (2, 1, 3, 0):
            at = x_rows(d, part)
            gu = dot_l(tokb[:, at], guh[h]).astype(BF16)
            dn = dot_l(gob[:, at], hdup[h])
            dwq[h, d, 0], dwq[h, d, 1] = gu[:hp], gu[hp:]
            dwq[h, d, 2] = jnp.where(ld, dn[:hp], dn[hp:]).astype(BF16)
            if d:
                for c in range(3):
                    cs[c].append(copy(dwq.at[h, d, c], dwqr.at[h, NX - d - 1, c], x_peer(d)))
        return cs

    def send_z(h, c, arrivals):
        for a in arrivals:
            a.wait_recv()
        total = dwq[h, 0, c].astype(F32)
        for n in range(NX - 1):
            total += dwqr[h, n, c].astype(F32)
        zsend[h, c] = total.astype(BF16)
        return copy(zsend.at[h, c], zrecv.at[h, c], z_peer)

    for c in x_r[0]:
        c.wait_recv()
    hidden_other(0)
    x_d1 = [grads_other(0), None]
    pass_on(4)
    for c in x_w:
        c.wait_recv()
    hidden_own()
    z_d = [send_z(0, 0, x_d1[0][0])]
    pass_on(5)
    for c in (1, 2):
        z_d.append(send_z(0, c, x_d1[0][c]))

    for c in x_r[1]:
        c.wait_recv()
    hidden_other(1)
    lall = low((hp, hidden))
    for s in range(NX):
        d0, d1 = rd[0, pl.ds(s * hp, hp)].astype(F32), rd[1, pl.ds(s * hp, hp)].astype(F32)
        rdn[pl.ds(s * part, hp)] = jnp.where(lall, d0, swap(d1)).astype(BF16)
        rdn[pl.ds(s * part + hp, hp)] = jnp.where(lall, swap(d0), d1).astype(BF16)
    lfull = low((NY * rows, hidden))
    hsb[1] = jnp.where(lfull, hdup[0].astype(F32), hdup[1].astype(F32)).astype(BF16)

    hs = jnp.concatenate([hsb[0], hsb[1]], axis=1)
    gu = jnp.concatenate([gub[0], gub[1]], axis=1)
    y_far = []
    for s in range(NX):
        cols = pl.ds(s * part, part)
        lop[:, cols] = dot_t(hs, jnp.concatenate([wb[2, cols], rdn[cols]], axis=1)).astype(BF16)
        both = jnp.concatenate([wb[0, cols], wb[1, cols], rw[0, cols], rw[1, cols]], axis=1)
        gtp[:, cols] = dot_t(gu, both).astype(BF16)
        for n, buf in enumerate((lop, gtp)):
            for m, d in enumerate((1, 3)):
                r0 = m * half
                c = copy(buf.at[pl.ds(2 * rows + r0, half), cols], far.at[n, m, :, cols], y_peer(d))
                y_far.append(c)
    y_g = [copy(gst.at[d], gsr.at[NY - d - 1], y_peer(d)) for d in (2, 1, 3)]
    y_o = []
    for buf, dst in ((lop, lor), (gtp, gtr)):
        for m, d in enumerate((1, 3)):
            r0 = half - m * half
            y_o.append(copy(buf.at[pl.ds(d * rows + r0, half)], dst.at[m, pl.ds(r0, half)], y_peer(d)))
    x_d1[1] = grads_other(1)
    k = 0
    for s in range(NX):
        cols = pl.ds(s * part, part)
        for n, (buf, dst) in enumerate(((lop, lor), (gtp, gtr))):
            for m, d in enumerate((1, 3)):
                r0 = m * half
                y_far[k].wait_recv()
                k += 1
                at = pl.ds(d * rows + r0, half)
                buf[at, cols] = (buf[at, cols].astype(F32) + far[n, m, :, cols].astype(F32)).astype(BF16)
                y_o.append(copy(buf.at[at, cols], dst.at[m, pl.ds(r0, half), cols], y_peer(d)))
        if s < 3:
            z_d.append(send_z(1, s, x_d1[1][s]))

    x_d0 = []
    for d in (2, 1, 3, 0):
        at = x_rows(d, part)
        both = dot_l(tokb[:, at], gub[0]).astype(BF16)
        dwb[d, 0], dwb[d, 1] = both[:, :hidden], both[:, hidden:]
        dwb[d, 2] = dot_l(gob[:, at], hsb[0]).astype(BF16)
        if d:
            for i in range(3):
                x_d0.append(copy(dwb.at[d, i], dwr.at[NX - d - 1, i], x_peer(d)))
    for c in x_d0:
        c.wait_recv()
    for i in range(3):
        total = dwb[0, i].astype(F32)
        for n in range(NX - 1):
            total += dwr[n, i].astype(F32)
        dout[i] = total

    outs = []
    for c in y_g + y_o:
        c.wait_recv()
    for n, (buf, got, out) in enumerate(((lop, lor, lo), (gtp, gtr, gt))):
        total = buf[slot(0)].astype(F32) + got[0].astype(F32) + got[1].astype(F32)
        buf[slot(0)] = total.astype(BF16)
        c = pltpu.make_async_copy(buf.at[slot(0)], out, out_sem.at[n])
        c.start()
        outs.append(c)
    gs_sum = gst[0] + gsr[0] + gsr[1] + gsr[2]
    for k in range(ids.shape[0]):
        gs[k : k + 1] = jnp.sum(jnp.where(sub == ids[k : k + 1], gs_sum, 0.0), axis=0, keepdims=True)

    for c in z_d:
        c.wait_recv()
    for c in range(2):
        at = pl.ds(c * hp, hp)
        p1, p2 = zrecv[0, c].astype(F32), zrecv[1, c].astype(F32)
        dout[0, at] += jnp.where(ld, p1, swap(p2))
        dout[1, at] += jnp.where(ld, swap(p1), p2)
    q1, q2 = zrecv[0, 2].astype(F32), zrecv[1, 2].astype(F32)
    dout[2, pl.ds(0, hp)] += jnp.where(ld, q1, swap(q2))
    dout[2, pl.ds(hp, hp)] += jnp.where(ld, swap(q1), q2)
    for i, out in enumerate((dg, du, dd)):
        c = pltpu.make_async_copy(dout.at[i], out, out_sem.at[2 + i])
        c.start()
        outs.append(c)
    for c in made:
        c.wait_send()
    for c in outs:
        c.wait()


def hand_on(*refs):
    n = (len(refs) - 2) // 3
    held, sem = refs[2 * n : 3 * n], refs[-2:]
    into = [pltpu.make_async_copy(refs[i], held[i], sem[0].at[i]) for i in range(n)]
    out = [pltpu.make_async_copy(held[i], refs[n + i], sem[1].at[i]) for i in range(n)]
    for c in into:
        c.start()
    for i in range(n):
        into[i].wait()
        out[i].start()
    for c in out:
        c.wait()


def local(tokens, expert_ids, gate_scores, gate_weight, up_weight, down_weight, grad_out):
    rows, width = tokens.shape
    _, part, hidden = gate_weight.shape
    top = expert_ids.shape[1]
    experts = lax.axis_size("expert")
    all_rows, half, hp = NY * rows, rows // 2, part // 2
    vmem, hbm = pl.BlockSpec(memory_space=pltpu.VMEM), pl.BlockSpec(memory_space=pl.ANY)
    shape = jax.ShapeDtypeStruct
    v = pltpu.VMEM
    scratch = [
        v((all_rows, width), BF16),
        v((all_rows, width), BF16),
        v((NY, experts, rows), F32),
        v((2, all_rows, hidden), F32),
        v((3, width, hidden), BF16),
        v((2, 3, hp, hidden), BF16),
        v((2, width, hidden), BF16),
        v((2, width // 2, hidden), BF16),
        v((width, hidden), BF16),
        v((all_rows, 2 * hidden), F32),
        v((all_rows, hidden), F32),
        v((all_rows, hidden), F32),
        v((2, all_rows, 2 * hidden), BF16),
        v((2, all_rows, hidden), BF16),
        v((2, all_rows, hidden), BF16),
        v((2, all_rows, hidden), BF16),
        v((NY, experts, rows), F32),
        v((NY - 1, experts, rows), F32),
        v((NX, 3, part, hidden), BF16),
        v((NX - 1, 3, part, hidden), BF16),
        v((2, NX, 3, hp, hidden), BF16),
        v((2, NX - 1, 3, hp, hidden), BF16),
        v((2, 3, hp, hidden), BF16),
        v((2, 3, hp, hidden), BF16),
        v((all_rows, width), BF16),
        v((all_rows, width), BF16),
        v((2, 2, half, width), BF16),
        v((2, rows, width), BF16),
        v((2, rows, width), BF16),
        v((3, part, hidden), F32),
        pltpu.SemaphoreType.DMA((N_COPIES,)),
        pltpu.SemaphoreType.DMA((N_COPIES,)),
        pltpu.SemaphoreType.DMA((5,)),
        pltpu.SemaphoreType.DMA((5,)),
    ]
    big, weight = shape((rows, width), BF16), shape((part, hidden), F32)
    shapes = [big, big, shape((top, rows), F32), weight, weight, weight]
    outs = pl.pallas_call(
        kernel,
        out_shape=shapes,
        in_specs=[hbm, hbm, vmem, vmem, hbm, hbm, hbm],
        out_specs=[hbm, hbm, vmem, hbm, hbm, hbm],
        scratch_shapes=scratch,
        compiler_params=pltpu.CompilerParams(
            collective_id=0, has_side_effects=True, vmem_limit_bytes=60 << 20
        ),
    )(tokens, grad_out, expert_ids.T, gate_scores.T, gate_weight[0], up_weight[0], down_weight[0])
    lo, gt, gs, dg, du, dd = pl.pallas_call(
        hand_on,
        out_shape=shapes,
        in_specs=[hbm] * 6,
        out_specs=[hbm] * 6,
        scratch_shapes=[v(o.shape, o.dtype) for o in shapes] + [pltpu.SemaphoreType.DMA((6,))] * 2,
    )(*outs)
    return lo, gt, gs.T, dg[None], du[None], dd[None]


def solution(mesh):
    rows_p = P(("section", "expert", "dp"), None)
    weight_p = P(("section", "expert"), "dp", None)
    return jax.shard_map(
        local,
        mesh=mesh,
        in_specs=(rows_p, rows_p, rows_p, weight_p, weight_p, weight_p, rows_p),
        out_specs=(rows_p, rows_p, rows_p, weight_p, weight_p, weight_p),
        check_vma=False,
    )
```

```python
import jax
import jax.numpy as jnp
from jax import lax
from jax.experimental import pallas as pl
from jax.experimental.pallas import tpu as pltpu
from jax.sharding import PartitionSpec as P

MESH = pl.DeviceIdType.MESH
F32 = jnp.float32
BF16 = jnp.bfloat16
NY = 4
NX = 4
N_COPIES = 192


def dot(a, b):
    return jnp.dot(a, b, preferred_element_type=F32)


def dot_t(a, b):
    return lax.dot_general(a, b, (((1,), (1,)), ((), ())), preferred_element_type=F32)


def dot_l(a, b):
    return lax.dot_general(a, b, (((0,), (0,)), ((), ())), preferred_element_type=F32)


def swap(a):
    return pltpu.roll(a.astype(F32), a.shape[1] // 2, axis=1)


def low(shape):
    return lax.broadcasted_iota(jnp.int32, shape, 1) < shape[1] // 2


def kernel(
    tok, go, ids, scores, wg, wu, wd,
    lo, gt, gs, dg, du, dd,
    tokb, gob, tab, sbc, wb, pk, rw, rd, rdn,
    pre, act, act2, gub, hsb, hdup, guh, gst, gsr,
    dwb, dwr, farw, dwq, dwqr, farq, zsend, zrecv, lop, gtp, far, lor, gtr, dout,
    send, recv, local_sem, out_sem,
):
    rows, width = tok.shape
    part, hidden = wg.shape
    half, hp, hq = rows // 2, part // 2, part // 4
    sec, ei, x = lax.axis_index("section"), lax.axis_index("expert"), lax.axis_index("dp")
    y, zh = ei // 2, ei % 2
    other = y * 2 + 1 - zh
    z_peer = (sec, other, x)

    def y_peer(d):
        return (sec, ((y + d) % NY) * 2 + zh, x)

    def x_peer(d):
        return (sec, ei, (x + d) % NX)

    peers = [z_peer] + [y_peer(d) for d in (1, 2, 3)] + [x_peer(d) for d in (1, 2, 3)]
    barrier = pltpu.get_barrier_semaphore()
    for p in peers:
        pl.semaphore_signal(barrier, inc=1, device_id=p, device_id_type=MESH)

    made = []

    def copy(src, dst, to):
        k = len(made)
        c = pltpu.make_async_remote_copy(
            src_ref=src, dst_ref=dst, send_sem=send.at[k], recv_sem=recv.at[k],
            device_id=to, device_id_type=MESH,
        )
        made.append(c)
        c.start()
        return c

    def x_rows(d, size):
        return pl.ds(pl.multiple_of(((x + d) % NX) * size, size), size)

    def slot(j):
        return pl.ds(j * rows, rows)

    mine = x_rows(0, part)
    w_in = (wg, wu, wd)
    own_w = [pltpu.make_async_copy(w_in[i], wb.at[i, mine], local_sem.at[i]) for i in range(3)]
    own_t = [pltpu.make_async_copy(tok, tokb.at[slot(0)], local_sem.at[3]),
             pltpu.make_async_copy(go, gob.at[slot(0)], local_sem.at[4])]
    for c in own_w + own_t:
        c.start()

    sub = lax.broadcasted_iota(jnp.int32, tab.shape[1:], 0)
    table = jnp.zeros(sub.shape, F32)
    for k in range(ids.shape[0]):
        table += jnp.where(sub == ids[k : k + 1], scores[k : k + 1], 0.0)
    tab[0] = table

    for c in own_w:
        c.wait()
    g, u, d = wb[0, mine].astype(F32), wb[1, mine].astype(F32), wb[2, mine].astype(F32)
    lw, ld = low((part, hidden)), low((hp, hidden))
    for h in range(2):
        if h == 0:
            gu = jnp.where(lw, g, swap(u)).astype(BF16)
            dn = jnp.where(ld, d[:hp], swap(d[hp:])).astype(BF16)
        else:
            gu = jnp.where(lw, swap(g), u).astype(BF16)
            dn = jnp.where(ld, swap(d[:hp]), d[hp:]).astype(BF16)
        pk[h, 0], pk[h, 1], pk[h, 2] = gu[:hp], gu[hp:], dn

    pl.semaphore_wait(barrier, len(peers))

    def unit(h, c, d=0, r0=0, size=hp):
        at = (x + d) % NX
        if c == 2:
            return rd.at[h, pl.ds(pl.multiple_of(at * hp + r0, hq), size)]
        return rw.at[h, pl.ds(pl.multiple_of(at * part + c * hp + r0, hq), size)]

    units = [(h, c) for h in range(2) for c in range(3)]
    z_w = [copy(pk.at[h, c], unit(h, c), z_peer) for h, c in units[:3]]
    y_s = [copy(tab.at[0], tab.at[NY - d], y_peer(d)) for d in (2, 1, 3)]
    bufs = ((tok, tokb), (go, gob))
    y_a, y_b = [], []
    for first in (True, False):
        for src, dst in bufs:
            for d in (1, 3):
                r0 = 0 if (d == 1) == first else half
                c = copy(src.at[pl.ds(r0, half)], dst.at[pl.ds((NY - d) * rows + r0, half)], y_peer(d))
                (y_a if first else y_b).append(c)
    x_a, x_w = [], []
    for first in (True, False):
        for i in range(3):
            for d in (1, 3):
                r0 = 0 if (d == 1) == first else hp
                at = pl.ds(pl.multiple_of(x * part + r0, hp), hp)
                c = copy(w_in[i].at[pl.ds(r0, hp)], wb.at[i, at], x_peer(d))
                (x_a if first else x_w).append(c)
    for i in range(3):
        for m, d in enumerate((1, 3)):
            x_a[2 * i + m].wait_recv()
            at = wb.at[i, pl.ds(pl.multiple_of(((x + NX - d) % NX) * part + m * hp, hp), hp)]
            x_w.append(copy(at, at, x_peer(d)))

    y_c = []
    for n, (_, dst) in enumerate(bufs):
        for m, d in enumerate((1, 3)):
            y_a[2 * n + m].wait_recv()
            r0 = 0 if d == 1 else half
            c = copy(dst.at[pl.ds((NY - d) * rows + r0, half)], dst.at[pl.ds(2 * rows + r0, half)], y_peer(d))
            y_c.append(c)

    x_n, x_r = [[] for _ in units], [[], []]

    def pass_on(n):
        z_w[n].wait_recv()
        for d in (1, 3):
            x_n[n].append(copy(unit(*units[n]), unit(*units[n]), x_peer(d)))

    def pass_far(n):
        for m, d in enumerate((1, 3)):
            x_n[n][m].wait_recv()
            at = unit(*units[n], NX - d, m * hq, hq)
            x_r[units[n][0]].append(copy(at, at, x_peer(d)))

    pass_on(0)
    pass_on(1)
    z_w += [copy(pk.at[h, c], unit(h, c), z_peer) for h, c in units[3:]]
    for c in y_s:
        c.wait_recv()
    for r, e in ((0, ei), (1, other)):
        for j in range(NY):
            row = jnp.sum(jnp.where(sub == e, tab[j], 0.0), axis=0, keepdims=True)
            sbc[r, slot(j)] = jnp.broadcast_to(row, (rows, hidden)).T
    pass_far(0)
    pass_on(2)
    pass_far(1)
    pass_far(2)
    for c in own_t:
        c.wait()
    for c in y_b + y_c:
        c.wait_recv()

    def add_score(j, e, col):
        flat = jnp.broadcast_to(col, (rows, hidden)).T[: sub.shape[0]]
        gst[j] += jnp.where(sub == e, flat, 0.0)

    for j in range(NY):
        gst[j] = jnp.zeros(sub.shape, F32)

    def hidden_own():
        pre[...] = dot(tokb[...], jnp.concatenate([wb[0], wb[1]], axis=1))
        act[...] = dot(gob[...], wb[2])

        def step(j, _):
            at = pl.ds(pl.multiple_of(j * rows, rows), rows)
            g, u, a, s = pre[at, :hidden], pre[at, hidden:], act[at], sbc[0, at]
            sig = jax.nn.sigmoid(g)
            silu = g * sig
            h = silu * u
            ga = s * a
            hsb[0, at] = (s * h).astype(BF16)
            gub[0, at, :hidden] = (ga * u * sig * (1.0 + g * (1.0 - sig))).astype(BF16)
            gub[0, at, hidden:] = (ga * silu).astype(BF16)
            add_score(j, ei, jnp.sum(h * a, axis=1, keepdims=True))
            return 0

        lax.fori_loop(0, NY, step, 0)

    lr = low((rows, hidden))

    def hidden_other(h):
        pre[:, :hidden] = dot(tokb[...], rw[h])
        for s in range(NX):
            dn = rd[h, pl.ds(s * hp, hp)]
            a1 = dot(gob[:, pl.ds(s * part, hp)], dn)
            a2 = dot(gob[:, pl.ds(s * part + hp, hp)], dn)
            if s == 0:
                act[...], act2[...] = a1, a2
            else:
                act[...] += a1
                act2[...] += a2

        def step(j, _):
            at = pl.ds(pl.multiple_of(j * rows, rows), rows)
            p, s = pre[at, :hidden], sbc[1, at]
            q = swap(p)
            g, u = jnp.where(lr, p, q), jnp.where(lr, q, p)
            a = act[at] + swap(act2[at])
            a = jnp.where(lr, a, swap(a))
            sig = jax.nn.sigmoid(g)
            silu = g * sig
            hid = silu * u
            ga = s * a
            hs = (s * hid).astype(BF16)
            hdup[h, at] = hs
            gu = jnp.where(lr, ga * u * sig * (1.0 + g * (1.0 - sig)), ga * silu)
            guh[h, at] = gu.astype(BF16)
            gub[1, at, h * hidden : (h + 1) * hidden] = gu.astype(BF16)
            add_score(j, other, jnp.sum(jnp.where(lr, hid * a, 0.0), axis=1, keepdims=True))
            return 0

        lax.fori_loop(0, NY, step, 0)

    def halves_out(src, far_at, got, d):
        if d == 2:
            return [copy(src.at[pl.ds(m * far_at.shape[1], far_at.shape[1])], far_at.at[m], x_peer(e))
                    for m, e in enumerate((1, 3))]
        m = 0 if d == 1 else 1
        n = far_at.shape[1]
        return [copy(src.at[pl.ds(n - m * n, n)], got.at[m, pl.ds(n - m * n, n)], x_peer(d))]

    def halves_on(src_of, far_at, got, waits):
        n = far_at.shape[1]
        cs = []
        for m, d in enumerate((1, 3)):
            waits[m].wait_recv()
            at = pl.ds(m * n, n)
            src = src_of(d)
            src[at] = (src[at].astype(F32) + far_at[m].astype(F32)).astype(BF16)
            cs.append(copy(src.at[at], got.at[m, at], x_peer(d)))
        return cs

    x_far, x_d1 = [[], []], [[[], [], []], [[], [], []]]

    def grads_other(h):
        for d in (2, 1, 3, 0):
            at = x_rows(d, part)
            gu = dot_l(tokb[:, at], guh[h]).astype(BF16)
            dn = dot_l(gob[:, at], hdup[h])
            dwq[h, d, 0], dwq[h, d, 1] = gu[:hp], gu[hp:]
            dwq[h, d, 2] = jnp.where(ld, dn[:hp], dn[hp:]).astype(BF16)
            if d:
                for c in range(3):
                    cs = halves_out(dwq.at[h, d, c], farq.at[h, c], dwqr.at[h, c], d)
                    if d == 2:
                        x_far[h].append(cs)
                    else:
                        x_d1[h][c] += cs

    def grads_on(h):
        for c in range(3):
            x_d1[h][c] += halves_on(lambda d: dwq.at[h, d, c], farq.at[h, c], dwqr.at[h, c], x_far[h][c])

    def send_z(h, c):
        for a in x_d1[h][c]:
            a.wait_recv()
        total = dwq[h, 0, c].astype(F32) + dwqr[h, c, 0].astype(F32) + dwqr[h, c, 1].astype(F32)
        zsend[h, c] = total.astype(BF16)
        return copy(zsend.at[h, c], zrecv.at[h, c], z_peer)

    for c in x_r[0]:
        c.wait_recv()
    for n in (3, 4, 5):
        pass_on(n)
    hidden_other(0)
    for n in (3, 4, 5):
        pass_far(n)
    grads_other(0)
    for c in x_w:
        c.wait_recv()
    hidden_own()
    grads_on(0)

    for c in x_r[1]:
        c.wait_recv()
    hidden_other(1)
    z_d = [send_z(0, c) for c in range(3)]
    lall = low((hp, hidden))
    for s in range(NX):
        d0, d1 = rd[0, pl.ds(s * hp, hp)].astype(F32), rd[1, pl.ds(s * hp, hp)].astype(F32)
        rdn[pl.ds(s * part, hp)] = jnp.where(lall, d0, swap(d1)).astype(BF16)
        rdn[pl.ds(s * part + hp, hp)] = jnp.where(lall, swap(d0), d1).astype(BF16)
    lfull = low((NY * rows, hidden))
    hsb[1] = jnp.where(lfull, hdup[0].astype(F32), hdup[1].astype(F32)).astype(BF16)

    hs = jnp.concatenate([hsb[0], hsb[1]], axis=1)
    gu = jnp.concatenate([gub[0], gub[1]], axis=1)
    y_far = []
    for s in range(NX):
        cols = pl.ds(s * part, part)
        lop[:, cols] = dot_t(hs, jnp.concatenate([wb[2, cols], rdn[cols]], axis=1)).astype(BF16)
        both = jnp.concatenate([wb[0, cols], wb[1, cols], rw[0, cols], rw[1, cols]], axis=1)
        gtp[:, cols] = dot_t(gu, both).astype(BF16)
        for n, buf in enumerate((lop, gtp)):
            for m, d in enumerate((1, 3)):
                r0 = m * half
                c = copy(buf.at[pl.ds(2 * rows + r0, half), cols], far.at[n, m, :, cols], y_peer(d))
                y_far.append(c)
    y_g = [copy(gst.at[d], gsr.at[NY - d - 1], y_peer(d)) for d in (2, 1, 3)]
    y_o = []
    for buf, dst in ((lop, lor), (gtp, gtr)):
        for m, d in enumerate((1, 3)):
            r0 = half - m * half
            y_o.append(copy(buf.at[pl.ds(d * rows + r0, half)], dst.at[m, pl.ds(r0, half)], y_peer(d)))
    grads_other(1)

    w_far, x_d0 = [], []
    for d in (2, 1, 3, 0):
        at = x_rows(d, part)
        both = dot_l(tokb[:, at], gub[0]).astype(BF16)
        dwb[d, 0], dwb[d, 1] = both[:, :hidden], both[:, hidden:]
        dwb[d, 2] = dot_l(gob[:, at], hsb[0]).astype(BF16)
        if d == 2:
            grads_on(1)
        if d:
            for i in range(3):
                cs = halves_out(dwb.at[d, i], farw.at[i], dwr.at[i], d)
                if d == 2:
                    w_far.append(cs)
                else:
                    x_d0 += cs

    for s in range(NX):
        cols = pl.ds(s * part, part)
        for n, (buf, dst) in enumerate(((lop, lor), (gtp, gtr))):
            for m, d in enumerate((1, 3)):
                r0 = m * half
                y_far[4 * s + 2 * n + m].wait_recv()
                at = pl.ds(d * rows + r0, half)
                buf[at, cols] = (buf[at, cols].astype(F32) + far[n, m, :, cols].astype(F32)).astype(BF16)
                y_o.append(copy(buf.at[at, cols], dst.at[m, pl.ds(r0, half), cols], y_peer(d)))
        if s == 2:
            z_d += [send_z(1, c) for c in range(3)]
    for i in range(3):
        x_d0 += halves_on(lambda d: dwb.at[d, i], farw.at[i], dwr.at[i], w_far[i])
    for c in x_d0:
        c.wait_recv()
    for i in range(3):
        dout[i] = dwb[0, i].astype(F32) + dwr[i, 0].astype(F32) + dwr[i, 1].astype(F32)

    outs = []
    for c in y_g + y_o[:4]:
        c.wait_recv()
    for s in range(NX):
        cols = pl.ds(s * part, part)
        for n, (buf, got, out) in enumerate(((lop, lor, lo), (gtp, gtr, gt))):
            for m in range(2):
                y_o[4 + 4 * s + 2 * n + m].wait_recv()
            total = buf[slot(0), cols].astype(F32) + got[0, :, cols].astype(F32) + got[1, :, cols].astype(F32)
            buf[slot(0), cols] = total.astype(BF16)
            c = pltpu.make_async_copy(buf.at[slot(0), cols], out.at[:, cols], out_sem.at[2 * s + n])
            c.start()
            outs.append(c)
    gs_sum = gst[0] + gsr[0] + gsr[1] + gsr[2]
    for k in range(ids.shape[0]):
        gs[k : k + 1] = jnp.sum(jnp.where(sub == ids[k : k + 1], gs_sum, 0.0), axis=0, keepdims=True)

    for c in z_d:
        c.wait_recv()
    for c in range(2):
        at = pl.ds(c * hp, hp)
        p1, p2 = zrecv[0, c].astype(F32), zrecv[1, c].astype(F32)
        dout[0, at] += jnp.where(ld, p1, swap(p2))
        dout[1, at] += jnp.where(ld, swap(p1), p2)
    q1, q2 = zrecv[0, 2].astype(F32), zrecv[1, 2].astype(F32)
    dout[2, pl.ds(0, hp)] += jnp.where(ld, q1, swap(q2))
    dout[2, pl.ds(hp, hp)] += jnp.where(ld, swap(q1), q2)
    for i, out in enumerate((dg, du, dd)):
        c = pltpu.make_async_copy(dout.at[i], out, out_sem.at[2 * NX + i])
        c.start()
        outs.append(c)
    for c in made:
        c.wait_send()
    for c in outs:
        c.wait()


def hand_on(*refs):
    n = (len(refs) - 2) // 3
    held, sem = refs[2 * n : 3 * n], refs[-2:]
    into = [pltpu.make_async_copy(refs[i], held[i], sem[0].at[i]) for i in range(n)]
    out = [pltpu.make_async_copy(held[i], refs[n + i], sem[1].at[i]) for i in range(n)]
    for c in into:
        c.start()
    for i in range(n):
        into[i].wait()
        out[i].start()
    for c in out:
        c.wait()


def local(tokens, expert_ids, gate_scores, gate_weight, up_weight, down_weight, grad_out):
    rows, width = tokens.shape
    _, part, hidden = gate_weight.shape
    top = expert_ids.shape[1]
    experts = lax.axis_size("expert")
    all_rows, half, hp = NY * rows, rows // 2, part // 2
    vmem, hbm = pl.BlockSpec(memory_space=pltpu.VMEM), pl.BlockSpec(memory_space=pl.ANY)
    shape = jax.ShapeDtypeStruct
    v = pltpu.VMEM
    scratch = [
        v((all_rows, width), BF16),
        v((all_rows, width), BF16),
        v((NY, experts, rows), F32),
        v((2, all_rows, hidden), F32),
        v((3, width, hidden), BF16),
        v((2, 3, hp, hidden), BF16),
        v((2, width, hidden), BF16),
        v((2, width // 2, hidden), BF16),
        v((width, hidden), BF16),
        v((all_rows, 2 * hidden), F32),
        v((all_rows, hidden), F32),
        v((all_rows, hidden), F32),
        v((2, all_rows, 2 * hidden), BF16),
        v((2, all_rows, hidden), BF16),
        v((2, all_rows, hidden), BF16),
        v((2, all_rows, hidden), BF16),
        v((NY, experts, rows), F32),
        v((NY - 1, experts, rows), F32),
        v((NX, 3, part, hidden), BF16),
        v((3, 2, part, hidden), BF16),
        v((3, 2, hp, hidden), BF16),
        v((2, NX, 3, hp, hidden), BF16),
        v((2, 3, 2, hp, hidden), BF16),
        v((2, 3, 2, hp // 2, hidden), BF16),
        v((2, 3, hp, hidden), BF16),
        v((2, 3, hp, hidden), BF16),
        v((all_rows, width), BF16),
        v((all_rows, width), BF16),
        v((2, 2, half, width), BF16),
        v((2, rows, width), BF16),
        v((2, rows, width), BF16),
        v((3, part, hidden), F32),
        pltpu.SemaphoreType.DMA((N_COPIES,)),
        pltpu.SemaphoreType.DMA((N_COPIES,)),
        pltpu.SemaphoreType.DMA((5,)),
        pltpu.SemaphoreType.DMA((2 * NX + 3,)),
    ]
    big, weight = shape((rows, width), BF16), shape((part, hidden), F32)
    shapes = [big, big, shape((top, rows), F32), weight, weight, weight]
    outs = pl.pallas_call(
        kernel,
        out_shape=shapes,
        in_specs=[hbm, hbm, vmem, vmem, hbm, hbm, hbm],
        out_specs=[hbm, hbm, vmem, hbm, hbm, hbm],
        scratch_shapes=scratch,
        compiler_params=pltpu.CompilerParams(
            collective_id=0, has_side_effects=True, vmem_limit_bytes=60 << 20
        ),
    )(tokens, grad_out, expert_ids.T, gate_scores.T, gate_weight[0], up_weight[0], down_weight[0])
    lo, gt, gs, dg, du, dd = pl.pallas_call(
        hand_on,
        out_shape=shapes,
        in_specs=[hbm] * 6,
        out_specs=[hbm] * 6,
        scratch_shapes=[v(o.shape, o.dtype) for o in shapes] + [pltpu.SemaphoreType.DMA((6,))] * 2,
    )(*outs)
    return lo, gt, gs.T, dg[None], du[None], dd[None]


def solution(mesh):
    rows_p = P(("section", "expert", "dp"), None)
    weight_p = P(("section", "expert"), "dp", None)
    return jax.shard_map(
        local,
        mesh=mesh,
        in_specs=(rows_p, rows_p, rows_p, weight_p, weight_p, weight_p, rows_p),
        out_specs=(rows_p, rows_p, rows_p, weight_p, weight_p, weight_p),
        check_vma=False,
    )
```

```python
import jax
import jax.numpy as jnp
from jax import lax
from jax.experimental import pallas as pl
from jax.experimental.pallas import tpu as pltpu
from jax.sharding import PartitionSpec as P

MESH = pl.DeviceIdType.MESH
F32 = jnp.float32
BF16 = jnp.bfloat16
NY = 4
NX = 4
N_COPIES = 192
FIRST = 5
PLACE = (0, 1, 3, 2)


def dot(a, b):
    return jnp.dot(a, b, preferred_element_type=F32)


def dot_t(a, b):
    return lax.dot_general(a, b, (((1,), (1,)), ((), ())), preferred_element_type=F32)


def dot_l(a, b):
    return lax.dot_general(a, b, (((0,), (0,)), ((), ())), preferred_element_type=F32)


def swap(a):
    return pltpu.roll(a.astype(F32), a.shape[1] // 2, axis=1)


def low(shape):
    return lax.broadcasted_iota(jnp.int32, shape, 1) < shape[1] // 2


def kernel(
    tok, go, ids, scores, wg, wu, wd,
    lo, gt, gs, dg, du, dd,
    tokb, gob, tab, sbc, wb, pk, rw, rd, rdn,
    pre, act, act2, gub, hsb, hdup, guh, gst, gsr,
    dwb, dwr, farw, dwq, dwqr, farq, zsend, zrecv, lop, gtp, far, lor, gtr, dout,
    send, recv, local_sem, out_sem,
):
    rows, width = tok.shape
    part, hidden = wg.shape
    half, hp, hq = rows // 2, part // 2, part // 4
    sec, ei, x = lax.axis_index("section"), lax.axis_index("expert"), lax.axis_index("dp")
    y, zh = ei // 2, ei % 2
    other = y * 2 + 1 - zh
    z_peer = (sec, other, x)

    def y_peer(d):
        return (sec, ((y + d) % NY) * 2 + zh, x)

    def x_peer(d):
        return (sec, ei, (x + d) % NX)

    peers = [z_peer] + [y_peer(d) for d in (1, 2, 3)] + [x_peer(d) for d in (1, 2, 3)]
    barrier = pltpu.get_barrier_semaphore()
    for p in peers:
        pl.semaphore_signal(barrier, inc=1, device_id=p, device_id_type=MESH)

    made = []

    def copy(src, dst, to):
        k = len(made)
        c = pltpu.make_async_remote_copy(
            src_ref=src, dst_ref=dst, send_sem=send.at[k], recv_sem=recv.at[k],
            device_id=to, device_id_type=MESH,
        )
        made.append(c)
        c.start()
        return c

    def x_rows(d, size):
        return pl.ds(pl.multiple_of(((x + d) % NX) * size, size), size)

    def slot(j, r0=0, size=rows):
        return pl.ds(PLACE[j] * rows + r0, size)

    mine = x_rows(0, part)
    w_in = (wg, wu, wd)
    own_w = [pltpu.make_async_copy(w_in[i], wb.at[i, mine], local_sem.at[i]) for i in range(3)]
    own_t = [pltpu.make_async_copy(tok, tokb.at[slot(0)], local_sem.at[3]),
             pltpu.make_async_copy(go, gob.at[slot(0)], local_sem.at[4])]
    for c in own_w + own_t:
        c.start()

    sub = lax.broadcasted_iota(jnp.int32, tab.shape[1:], 0)
    table = jnp.zeros(sub.shape, F32)
    for k in range(ids.shape[0]):
        table += jnp.where(sub == ids[k : k + 1], scores[k : k + 1], 0.0)
    tab[0] = table

    for c in own_w:
        c.wait()
    g, u, d = wb[0, mine].astype(F32), wb[1, mine].astype(F32), wb[2, mine].astype(F32)
    lw, ld = low((part, hidden)), low((hp, hidden))
    for h in range(2):
        if h == 0:
            gu = jnp.where(lw, g, swap(u)).astype(BF16)
            dn = jnp.where(ld, d[:hp], swap(d[hp:])).astype(BF16)
        else:
            gu = jnp.where(lw, swap(g), u).astype(BF16)
            dn = jnp.where(ld, swap(d[:hp]), d[hp:]).astype(BF16)
        pk[h, 0], pk[h, 1], pk[h, 2] = gu[:hp], gu[hp:], dn

    pl.semaphore_wait(barrier, len(peers))

    def unit(h, c, d=0, r0=0, size=hp):
        at = (x + d) % NX
        if c == 2:
            return rd.at[h, pl.ds(pl.multiple_of(at * hp + r0, hq), size)]
        return rw.at[h, pl.ds(pl.multiple_of(at * part + c * hp + r0, hq), size)]

    units = [(h, c) for h in range(2) for c in range(3)]
    z_w = [copy(pk.at[h, c], unit(h, c), z_peer) for h, c in units[:FIRST]]
    y_s = [copy(tab.at[0], tab.at[PLACE[NY - d]], y_peer(d)) for d in (2, 1, 3)]
    bufs = ((tok, tokb), (go, gob))
    y_a, y_b = [], []
    for first in (True, False):
        for src, dst in bufs:
            for d in (1, 3):
                r0 = 0 if (d == 1) == first else half
                c = copy(src.at[pl.ds(r0, half)], dst.at[slot(NY - d, r0, half)], y_peer(d))
                (y_a if first else y_b).append(c)
    x_a, x_w = [], []
    for first in (True, False):
        for i in range(3):
            for d in (1, 3):
                r0 = 0 if (d == 1) == first else hp
                at = pl.ds(pl.multiple_of(x * part + r0, hp), hp)
                c = copy(w_in[i].at[pl.ds(r0, hp)], wb.at[i, at], x_peer(d))
                (x_a if first else x_w).append(c)
    for i in range(3):
        for m, d in enumerate((1, 3)):
            x_a[2 * i + m].wait_recv()
            at = wb.at[i, pl.ds(pl.multiple_of(((x + NX - d) % NX) * part + m * hp, hp), hp)]
            x_w.append(copy(at, at, x_peer(d)))

    y_c = []
    for n, (_, dst) in enumerate(bufs):
        for m, d in enumerate((1, 3)):
            y_a[2 * n + m].wait_recv()
            r0 = 0 if d == 1 else half
            c = copy(dst.at[slot(NY - d, r0, half)], dst.at[slot(2, r0, half)], y_peer(d))
            y_c.append(c)

    x_n, x_r = [[] for _ in units], [[], []]

    def pass_on(n):
        z_w[n].wait_recv()
        for d in (1, 3):
            x_n[n].append(copy(unit(*units[n]), unit(*units[n]), x_peer(d)))

    def pass_far(n):
        for m, d in enumerate((1, 3)):
            x_n[n][m].wait_recv()
            at = unit(*units[n], NX - d, m * hq, hq)
            x_r[units[n][0]].append(copy(at, at, x_peer(d)))

    pass_on(0)
    pass_on(1)
    z_w += [copy(pk.at[h, c], unit(h, c), z_peer) for h, c in units[FIRST:]]
    for c in y_s:
        c.wait_recv()
    for r, e in ((0, ei), (1, other)):
        for j in range(NY):
            row = jnp.sum(jnp.where(sub == e, tab[j], 0.0), axis=0, keepdims=True)
            sbc[r, pl.ds(j * rows, rows)] = jnp.broadcast_to(row, (rows, hidden)).T
    pass_far(0)
    pass_on(2)
    pass_far(1)
    pass_on(3)
    pass_far(2)
    pass_far(3)
    for c in own_t:
        c.wait()
    for c in y_b:
        c.wait_recv()

    def add_score(j, e, col):
        flat = jnp.broadcast_to(col, (rows, hidden)).T[: sub.shape[0]]
        gst[j] += jnp.where(sub == e, flat, 0.0)

    for j in range(NY):
        gst[j] = jnp.zeros(sub.shape, F32)

    def hidden_own(j0, j1):
        every = pl.ds(j0 * rows, (j1 - j0) * rows)
        pre[every] = dot(tokb[every], jnp.concatenate([wb[0], wb[1]], axis=1))
        act[every] = dot(gob[every], wb[2])

        def step(j, _):
            at = pl.ds(pl.multiple_of(j * rows, rows), rows)
            g, u, a, s = pre[at, :hidden], pre[at, hidden:], act[at], sbc[0, at]
            sig = jax.nn.sigmoid(g)
            silu = g * sig
            h = silu * u
            ga = s * a
            hsb[0, at] = (s * h).astype(BF16)
            gub[0, at, :hidden] = (ga * u * sig * (1.0 + g * (1.0 - sig))).astype(BF16)
            gub[0, at, hidden:] = (ga * silu).astype(BF16)
            add_score(j, ei, jnp.sum(h * a, axis=1, keepdims=True))
            return 0

        lax.fori_loop(j0, j1, step, 0)

    lr = low((rows, hidden))

    def hidden_other(h, j0, j1):
        every = pl.ds(j0 * rows, (j1 - j0) * rows)
        pre[every, :hidden] = dot(tokb[every], rw[h])
        for s in range(NX):
            dn = rd[h, pl.ds(s * hp, hp)]
            a1 = dot(gob[every, pl.ds(s * part, hp)], dn)
            a2 = dot(gob[every, pl.ds(s * part + hp, hp)], dn)
            if s == 0:
                act[every], act2[every] = a1, a2
            else:
                act[every] += a1
                act2[every] += a2

        def step(j, _):
            at = pl.ds(pl.multiple_of(j * rows, rows), rows)
            p, s = pre[at, :hidden], sbc[1, at]
            q = swap(p)
            g, u = jnp.where(lr, p, q), jnp.where(lr, q, p)
            a = act[at] + swap(act2[at])
            a = jnp.where(lr, a, swap(a))
            sig = jax.nn.sigmoid(g)
            silu = g * sig
            hid = silu * u
            ga = s * a
            hs = (s * hid).astype(BF16)
            hdup[h, at] = hs
            gu = jnp.where(lr, ga * u * sig * (1.0 + g * (1.0 - sig)), ga * silu)
            guh[h, at] = gu.astype(BF16)
            gub[1, at, h * hidden : (h + 1) * hidden] = gu.astype(BF16)
            add_score(j, other, jnp.sum(jnp.where(lr, hid * a, 0.0), axis=1, keepdims=True))
            return 0

        lax.fori_loop(j0, j1, step, 0)

    def halves_out(src, far_at, got, d):
        if d == 2:
            return [copy(src.at[pl.ds(m * far_at.shape[1], far_at.shape[1])], far_at.at[m], x_peer(e))
                    for m, e in enumerate((1, 3))]
        m = 0 if d == 1 else 1
        n = far_at.shape[1]
        return [copy(src.at[pl.ds(n - m * n, n)], got.at[m, pl.ds(n - m * n, n)], x_peer(d))]

    def halves_on(src_of, far_at, got, waits):
        n = far_at.shape[1]
        cs = []
        for m, d in enumerate((1, 3)):
            waits[m].wait_recv()
            at = pl.ds(m * n, n)
            src = src_of(d)
            src[at] = (src[at].astype(F32) + far_at[m].astype(F32)).astype(BF16)
            cs.append(copy(src.at[at], got.at[m, at], x_peer(d)))
        return cs

    x_far, x_d1 = [[], []], [[[], [], []], [[], [], []]]

    def grads_other(h):
        for d in (2, 1, 3, 0):
            at = x_rows(d, part)
            gu = dot_l(tokb[:, at], guh[h]).astype(BF16)
            dn = dot_l(gob[:, at], hdup[h])
            dwq[h, d, 0], dwq[h, d, 1] = gu[:hp], gu[hp:]
            dwq[h, d, 2] = jnp.where(ld, dn[:hp], dn[hp:]).astype(BF16)

    def grads_out(h, c):
        x_far[h].append(halves_out(dwq.at[h, 2, c], farq.at[h, c], dwqr.at[h, c], 2))
        for d in (1, 3):
            x_d1[h][c] += halves_out(dwq.at[h, d, c], farq.at[h, c], dwqr.at[h, c], d)

    def grads_on(h, c):
        x_d1[h][c] += halves_on(lambda d: dwq.at[h, d, c], farq.at[h, c], dwqr.at[h, c], x_far[h][c])

    def send_z(h, c):
        for a in x_d1[h][c]:
            a.wait_recv()
        total = dwq[h, 0, c].astype(F32) + dwqr[h, c, 0].astype(F32) + dwqr[h, c, 1].astype(F32)
        zsend[h, c] = total.astype(BF16)
        return copy(zsend.at[h, c], zrecv.at[h, c], z_peer)

    for c in x_w:
        c.wait_recv()
    hidden_own(0, 3)
    for c in x_r[0]:
        c.wait_recv()
    hidden_other(0, 0, 3)
    for c in y_c:
        c.wait_recv()
    pass_on(4)
    hidden_other(0, 3, 4)
    pass_on(5)
    pass_far(4)
    grads_other(0)
    pass_far(5)
    grads_out(0, 0)
    hidden_own(3, 4)
    grads_on(0, 0)

    for c in x_r[1]:
        c.wait_recv()
    grads_out(0, 1)
    grads_out(0, 2)
    hidden_other(1, 0, NY)
    z_d = [send_z(0, 0)]
    grads_on(0, 1)
    grads_on(0, 2)
    lall = low((hp, hidden))
    for s in range(NX):
        d0, d1 = rd[0, pl.ds(s * hp, hp)].astype(F32), rd[1, pl.ds(s * hp, hp)].astype(F32)
        rdn[pl.ds(s * part, hp)] = jnp.where(lall, d0, swap(d1)).astype(BF16)
        rdn[pl.ds(s * part + hp, hp)] = jnp.where(lall, swap(d0), d1).astype(BF16)
    lfull = low((NY * rows, hidden))
    hsb[1] = jnp.where(lfull, hdup[0].astype(F32), hdup[1].astype(F32)).astype(BF16)

    hs = jnp.concatenate([hsb[0], hsb[1]], axis=1)
    gu = jnp.concatenate([gub[0], gub[1]], axis=1)
    y_far = []
    for s in range(NX):
        cols = pl.ds(s * part, part)
        lop[:, cols] = dot_t(hs, jnp.concatenate([wb[2, cols], rdn[cols]], axis=1)).astype(BF16)
        both = jnp.concatenate([wb[0, cols], wb[1, cols], rw[0, cols], rw[1, cols]], axis=1)
        gtp[:, cols] = dot_t(gu, both).astype(BF16)
        for n, buf in enumerate((lop, gtp)):
            for m, d in enumerate((1, 3)):
                r0 = m * half
                c = copy(buf.at[slot(2, r0, half), cols], far.at[n, m, :, cols], y_peer(d))
                y_far.append(c)
        if s in (1, 2):
            z_d.append(send_z(0, s))
    y_g = [copy(gst.at[PLACE[d]], gsr.at[NY - d - 1], y_peer(d)) for d in (2, 1, 3)]
    y_o = []
    for buf, dst in ((lop, lor), (gtp, gtr)):
        for m, d in enumerate((1, 3)):
            r0 = half - m * half
            y_o.append(copy(buf.at[slot(d, r0, half)], dst.at[m, pl.ds(r0, half)], y_peer(d)))
    grads_other(1)
    for c in range(3):
        grads_out(1, c)

    for d in (2, 1, 3, 0):
        at = x_rows(d, part)
        both = dot_l(tokb[:, at], gub[0]).astype(BF16)
        dwb[d, 0], dwb[d, 1] = both[:, :hidden], both[:, hidden:]
        dwb[d, 2] = dot_l(gob[:, at], hsb[0]).astype(BF16)
    for c in range(3):
        grads_on(1, c)
    z_d += [send_z(1, c) for c in range(3)]
    w_far, x_d0 = [], []
    for i in range(3):
        w_far.append(halves_out(dwb.at[2, i], farw.at[i], dwr.at[i], 2))
    for i in range(3):
        for d in (1, 3):
            x_d0 += halves_out(dwb.at[d, i], farw.at[i], dwr.at[i], d)

    for s in range(NX):
        cols = pl.ds(s * part, part)
        for n, (buf, dst) in enumerate(((lop, lor), (gtp, gtr))):
            for m, d in enumerate((1, 3)):
                r0 = m * half
                y_far[4 * s + 2 * n + m].wait_recv()
                at = slot(d, r0, half)
                buf[at, cols] = (buf[at, cols].astype(F32) + far[n, m, :, cols].astype(F32)).astype(BF16)
                y_o.append(copy(buf.at[at, cols], dst.at[m, pl.ds(r0, half), cols], y_peer(d)))
    for i in range(3):
        x_d0 += halves_on(lambda d: dwb.at[d, i], farw.at[i], dwr.at[i], w_far[i])
    for c in x_d0:
        c.wait_recv()
    for i in range(3):
        dout[i] = dwb[0, i].astype(F32) + dwr[i, 0].astype(F32) + dwr[i, 1].astype(F32)

    outs = []
    for c in y_g + y_o[:4]:
        c.wait_recv()
    for s in range(NX):
        cols = pl.ds(s * part, part)
        for n, (buf, got, out) in enumerate(((lop, lor, lo), (gtp, gtr, gt))):
            for m in range(2):
                y_o[4 + 4 * s + 2 * n + m].wait_recv()
            total = buf[slot(0), cols].astype(F32) + got[0, :, cols].astype(F32) + got[1, :, cols].astype(F32)
            buf[slot(0), cols] = total.astype(BF16)
            c = pltpu.make_async_copy(buf.at[slot(0), cols], out.at[:, cols], out_sem.at[2 * s + n])
            c.start()
            outs.append(c)
    gs_sum = gst[0] + gsr[0] + gsr[1] + gsr[2]
    for k in range(ids.shape[0]):
        gs[k : k + 1] = jnp.sum(jnp.where(sub == ids[k : k + 1], gs_sum, 0.0), axis=0, keepdims=True)

    for c in range(2):
        z_d[c].wait_recv()
        z_d[3 + c].wait_recv()
        at = pl.ds(c * hp, hp)
        p1, p2 = zrecv[0, c].astype(F32), zrecv[1, c].astype(F32)
        dout[0, at] += jnp.where(ld, p1, swap(p2))
        dout[1, at] += jnp.where(ld, swap(p1), p2)
    for i, out in enumerate((dg, du, dd)):
        if i == 2:
            z_d[2].wait_recv()
            z_d[5].wait_recv()
            q1, q2 = zrecv[0, 2].astype(F32), zrecv[1, 2].astype(F32)
            dout[2, pl.ds(0, hp)] += jnp.where(ld, q1, swap(q2))
            dout[2, pl.ds(hp, hp)] += jnp.where(ld, swap(q1), q2)
        c = pltpu.make_async_copy(dout.at[i], out, out_sem.at[2 * NX + i])
        c.start()
        outs.append(c)
    for c in made:
        c.wait_send()
    for c in outs:
        c.wait()


def hand_on(*refs):
    n = (len(refs) - 2) // 3
    held, sem = refs[2 * n : 3 * n], refs[-2:]
    into = [pltpu.make_async_copy(refs[i], held[i], sem[0].at[i]) for i in range(n)]
    out = [pltpu.make_async_copy(held[i], refs[n + i], sem[1].at[i]) for i in range(n)]
    for c in into:
        c.start()
    for i in range(n):
        into[i].wait()
        out[i].start()
    for c in out:
        c.wait()


def local(tokens, expert_ids, gate_scores, gate_weight, up_weight, down_weight, grad_out):
    rows, width = tokens.shape
    _, part, hidden = gate_weight.shape
    top = expert_ids.shape[1]
    experts = lax.axis_size("expert")
    all_rows, half, hp = NY * rows, rows // 2, part // 2
    vmem, hbm = pl.BlockSpec(memory_space=pltpu.VMEM), pl.BlockSpec(memory_space=pl.ANY)
    shape = jax.ShapeDtypeStruct
    v = pltpu.VMEM
    scratch = [
        v((all_rows, width), BF16),
        v((all_rows, width), BF16),
        v((NY, experts, rows), F32),
        v((2, all_rows, hidden), F32),
        v((3, width, hidden), BF16),
        v((2, 3, hp, hidden), BF16),
        v((2, width, hidden), BF16),
        v((2, width // 2, hidden), BF16),
        v((width, hidden), BF16),
        v((all_rows, 2 * hidden), F32),
        v((all_rows, hidden), F32),
        v((all_rows, hidden), F32),
        v((2, all_rows, 2 * hidden), BF16),
        v((2, all_rows, hidden), BF16),
        v((2, all_rows, hidden), BF16),
        v((2, all_rows, hidden), BF16),
        v((NY, experts, rows), F32),
        v((NY - 1, experts, rows), F32),
        v((NX, 3, part, hidden), BF16),
        v((3, 2, part, hidden), BF16),
        v((3, 2, hp, hidden), BF16),
        v((2, NX, 3, hp, hidden), BF16),
        v((2, 3, 2, hp, hidden), BF16),
        v((2, 3, 2, hp // 2, hidden), BF16),
        v((2, 3, hp, hidden), BF16),
        v((2, 3, hp, hidden), BF16),
        v((all_rows, width), BF16),
        v((all_rows, width), BF16),
        v((2, 2, half, width), BF16),
        v((2, rows, width), BF16),
        v((2, rows, width), BF16),
        v((3, part, hidden), F32),
        pltpu.SemaphoreType.DMA((N_COPIES,)),
        pltpu.SemaphoreType.DMA((N_COPIES,)),
        pltpu.SemaphoreType.DMA((5,)),
        pltpu.SemaphoreType.DMA((2 * NX + 3,)),
    ]
    big, weight = shape((rows, width), BF16), shape((part, hidden), F32)
    shapes = [big, big, shape((top, rows), F32), weight, weight, weight]
    outs = pl.pallas_call(
        kernel,
        out_shape=shapes,
        in_specs=[hbm, hbm, vmem, vmem, hbm, hbm, hbm],
        out_specs=[hbm, hbm, vmem, hbm, hbm, hbm],
        scratch_shapes=scratch,
        compiler_params=pltpu.CompilerParams(
            collective_id=0, has_side_effects=True, vmem_limit_bytes=60 << 20
        ),
    )(tokens, grad_out, expert_ids.T, gate_scores.T, gate_weight[0], up_weight[0], down_weight[0])
    lo, gt, gs, dg, du, dd = pl.pallas_call(
        hand_on,
        out_shape=shapes,
        in_specs=[hbm] * 6,
        out_specs=[hbm] * 6,
        scratch_shapes=[v(o.shape, o.dtype) for o in shapes] + [pltpu.SemaphoreType.DMA((6,))] * 2,
    )(*outs)
    return lo, gt, gs.T, dg[None], du[None], dd[None]


def solution(mesh):
    rows_p = P(("section", "expert", "dp"), None)
    weight_p = P(("section", "expert"), "dp", None)
    return jax.shard_map(
        local,
        mesh=mesh,
        in_specs=(rows_p, rows_p, rows_p, weight_p, weight_p, weight_p, rows_p),
        out_specs=(rows_p, rows_p, rows_p, weight_p, weight_p, weight_p),
        check_vma=False,
    )
```

```python
import jax
import jax.numpy as jnp
from jax import lax
from jax.experimental import pallas as pl
from jax.experimental.pallas import tpu as pltpu
from jax.sharding import PartitionSpec as P

MESH = pl.DeviceIdType.MESH
F32 = jnp.float32
BF16 = jnp.bfloat16
NY = 4
NX = 4
N_COPIES = 192
FIRST = 5
PLACE = (0, 1, 3, 2)


def dot(a, b):
    return jnp.dot(a, b, preferred_element_type=F32)


def dot_t(a, b):
    return lax.dot_general(a, b, (((1,), (1,)), ((), ())), preferred_element_type=F32)


def dot_l(a, b):
    return lax.dot_general(a, b, (((0,), (0,)), ((), ())), preferred_element_type=F32)


def swap(a):
    return pltpu.roll(a.astype(F32), a.shape[1] // 2, axis=1)


def low(shape):
    return lax.broadcasted_iota(jnp.int32, shape, 1) < shape[1] // 2


def kernel(
    tok, go, ids, scores, wg, wu, wd,
    lo, gt, gs, dg, du, dd,
    tokb, gob, tab, sbc, wb, pk, rw, rd, rdn,
    pre, act, act2, gub, hsb, hdup, guh, gst, gsr,
    dwb, dwr, farw, dwq, dwqr, farq, zsend, zrecv, lop, gtp, far, lor, gtr, dout,
    send, recv, local_sem, out_sem,
):
    rows, width = tok.shape
    part, hidden = wg.shape
    half, hp, hq = rows // 2, part // 2, part // 4
    sec, ei, x = lax.axis_index("section"), lax.axis_index("expert"), lax.axis_index("dp")
    y, zh = ei // 2, ei % 2
    other = y * 2 + 1 - zh
    z_peer = (sec, other, x)

    def y_peer(d):
        return (sec, ((y + d) % NY) * 2 + zh, x)

    def x_peer(d):
        return (sec, ei, (x + d) % NX)

    peers = [z_peer] + [y_peer(d) for d in (1, 2, 3)] + [x_peer(d) for d in (1, 2, 3)]
    barrier = pltpu.get_barrier_semaphore()
    for p in peers:
        pl.semaphore_signal(barrier, inc=1, device_id=p, device_id_type=MESH)

    made = []

    def copy(src, dst, to):
        k = len(made)
        c = pltpu.make_async_remote_copy(
            src_ref=src, dst_ref=dst, send_sem=send.at[k], recv_sem=recv.at[k],
            device_id=to, device_id_type=MESH,
        )
        made.append(c)
        c.start()
        return c

    def x_rows(d, size):
        return pl.ds(pl.multiple_of(((x + d) % NX) * size, size), size)

    def slot(j, r0=0, size=rows):
        return pl.ds(PLACE[j] * rows + r0, size)

    mine = x_rows(0, part)
    w_in = (wg, wu, wd)
    own_w = [pltpu.make_async_copy(w_in[i], wb.at[i, mine], local_sem.at[i]) for i in range(3)]
    own_t = [pltpu.make_async_copy(tok, tokb.at[slot(0)], local_sem.at[3]),
             pltpu.make_async_copy(go, gob.at[slot(0)], local_sem.at[4])]
    for c in own_w + own_t:
        c.start()

    sub = lax.broadcasted_iota(jnp.int32, tab.shape[1:], 0)
    table = jnp.zeros(sub.shape, F32)
    for k in range(ids.shape[0]):
        table += jnp.where(sub == ids[k : k + 1], scores[k : k + 1], 0.0)
    tab[0] = table

    for c in own_w:
        c.wait()
    g, u, d = wb[0, mine].astype(F32), wb[1, mine].astype(F32), wb[2, mine].astype(F32)
    lw, ld = low((part, hidden)), low((hp, hidden))
    for h in range(2):
        if h == 0:
            gu = jnp.where(lw, g, swap(u)).astype(BF16)
            dn = jnp.where(ld, d[:hp], swap(d[hp:])).astype(BF16)
        else:
            gu = jnp.where(lw, swap(g), u).astype(BF16)
            dn = jnp.where(ld, swap(d[:hp]), d[hp:]).astype(BF16)
        pk[h, 0], pk[h, 1], pk[h, 2] = gu[:hp], gu[hp:], dn

    pl.semaphore_wait(barrier, len(peers))

    def unit(h, c, d=0, r0=0, size=hp):
        at = (x + d) % NX
        if c == 2:
            return rd.at[h, pl.ds(pl.multiple_of(at * hp + r0, hq), size)]
        return rw.at[h, pl.ds(pl.multiple_of(at * part + c * hp + r0, hq), size)]

    units = [(h, c) for h in range(2) for c in range(3)]
    z_w = [copy(pk.at[h, c], unit(h, c), z_peer) for h, c in units[:FIRST]]
    y_s = [copy(tab.at[0], tab.at[PLACE[NY - d]], y_peer(d)) for d in (2, 1, 3)]
    bufs = ((tok, tokb), (go, gob))
    y_a, y_b = [], []
    for first in (True, False):
        for src, dst in bufs:
            for d in (1, 3):
                r0 = 0 if (d == 1) == first else half
                c = copy(src.at[pl.ds(r0, half)], dst.at[slot(NY - d, r0, half)], y_peer(d))
                (y_a if first else y_b).append(c)
    x_a, x_w = [], []
    for first in (True, False):
        for i in range(3):
            for d in (1, 3):
                r0 = 0 if (d == 1) == first else hp
                at = pl.ds(pl.multiple_of(x * part + r0, hp), hp)
                c = copy(w_in[i].at[pl.ds(r0, hp)], wb.at[i, at], x_peer(d))
                (x_a if first else x_w).append(c)
    for i in range(3):
        for m, d in enumerate((1, 3)):
            x_a[2 * i + m].wait_recv()
            at = wb.at[i, pl.ds(pl.multiple_of(((x + NX - d) % NX) * part + m * hp, hp), hp)]
            x_w.append(copy(at, at, x_peer(d)))

    y_c = []
    for n, (_, dst) in enumerate(bufs):
        for m, d in enumerate((1, 3)):
            y_a[2 * n + m].wait_recv()
            r0 = 0 if d == 1 else half
            c = copy(dst.at[slot(NY - d, r0, half)], dst.at[slot(2, r0, half)], y_peer(d))
            y_c.append(c)

    x_n, x_r = [[] for _ in units], [[], []]

    def pass_on(n):
        z_w[n].wait_recv()
        for d in (1, 3):
            x_n[n].append(copy(unit(*units[n]), unit(*units[n]), x_peer(d)))

    def pass_far(n):
        for m, d in enumerate((1, 3)):
            x_n[n][m].wait_recv()
            at = unit(*units[n], NX - d, m * hq, hq)
            x_r[units[n][0]].append(copy(at, at, x_peer(d)))

    pass_on(0)
    pass_on(1)
    z_w += [copy(pk.at[h, c], unit(h, c), z_peer) for h, c in units[FIRST:]]
    for c in y_s:
        c.wait_recv()
    for r, e in ((0, ei), (1, other)):
        for j in range(NY):
            row = jnp.sum(jnp.where(sub == e, tab[j], 0.0), axis=0, keepdims=True)
            sbc[r, pl.ds(j * rows, rows)] = jnp.broadcast_to(row, (rows, hidden)).T
    pass_far(0)
    pass_on(2)
    pass_far(1)
    pass_on(3)
    pass_far(2)
    pass_far(3)
    for c in own_t:
        c.wait()
    for c in y_b:
        c.wait_recv()

    def add_score(j, e, col):
        flat = jnp.broadcast_to(col, (rows, hidden)).T[: sub.shape[0]]
        gst[j] += jnp.where(sub == e, flat, 0.0)

    for j in range(NY):
        gst[j] = jnp.zeros(sub.shape, F32)

    def hidden_own(j0, j1):
        every = pl.ds(j0 * rows, (j1 - j0) * rows)
        pre[every] = dot(tokb[every], jnp.concatenate([wb[0], wb[1]], axis=1))
        act[every] = dot(gob[every], wb[2])

        def step(j, _):
            at = pl.ds(pl.multiple_of(j * rows, rows), rows)
            g, u, a, s = pre[at, :hidden], pre[at, hidden:], act[at], sbc[0, at]
            sig = jax.nn.sigmoid(g)
            silu = g * sig
            h = silu * u
            ga = s * a
            hsb[0, at] = (s * h).astype(BF16)
            gub[0, at, :hidden] = (ga * u * sig * (1.0 + g * (1.0 - sig))).astype(BF16)
            gub[0, at, hidden:] = (ga * silu).astype(BF16)
            add_score(j, ei, jnp.sum(h * a, axis=1, keepdims=True))
            return 0

        lax.fori_loop(j0, j1, step, 0)

    lr = low((rows, hidden))

    def hidden_other(h, j0, j1):
        every = pl.ds(j0 * rows, (j1 - j0) * rows)
        pre[every, :hidden] = dot(tokb[every], rw[h])
        for s in range(NX):
            dn = rd[h, pl.ds(s * hp, hp)]
            a1 = dot(gob[every, pl.ds(s * part, hp)], dn)
            a2 = dot(gob[every, pl.ds(s * part + hp, hp)], dn)
            if s == 0:
                act[every], act2[every] = a1, a2
            else:
                act[every] += a1
                act2[every] += a2

        def step(j, _):
            at = pl.ds(pl.multiple_of(j * rows, rows), rows)
            p, s = pre[at, :hidden], sbc[1, at]
            q = swap(p)
            g, u = jnp.where(lr, p, q), jnp.where(lr, q, p)
            a = act[at] + swap(act2[at])
            a = jnp.where(lr, a, swap(a))
            sig = jax.nn.sigmoid(g)
            silu = g * sig
            hid = silu * u
            ga = s * a
            hs = (s * hid).astype(BF16)
            hdup[h, at] = hs
            gu = jnp.where(lr, ga * u * sig * (1.0 + g * (1.0 - sig)), ga * silu)
            guh[h, at] = gu.astype(BF16)
            gub[1, at, h * hidden : (h + 1) * hidden] = gu.astype(BF16)
            add_score(j, other, jnp.sum(jnp.where(lr, hid * a, 0.0), axis=1, keepdims=True))
            return 0

        lax.fori_loop(j0, j1, step, 0)

    def halves_out(src, far_at, got, d):
        if d == 2:
            return [copy(src.at[pl.ds(m * far_at.shape[1], far_at.shape[1])], far_at.at[m], x_peer(e))
                    for m, e in enumerate((1, 3))]
        m = 0 if d == 1 else 1
        n = far_at.shape[1]
        return [copy(src.at[pl.ds(n - m * n, n)], got.at[m, pl.ds(n - m * n, n)], x_peer(d))]

    def halves_on(src_of, far_at, got, waits):
        n = far_at.shape[1]
        cs = []
        for m, d in enumerate((1, 3)):
            waits[m].wait_recv()
            at = pl.ds(m * n, n)
            src = src_of(d)
            src[at] = (src[at].astype(F32) + far_at[m].astype(F32)).astype(BF16)
            cs.append(copy(src.at[at], got.at[m, at], x_peer(d)))
        return cs

    x_far, x_d1 = [[], []], [[[], [], []], [[], [], []]]

    def grads_other(h):
        for d in (2, 1, 3, 0):
            at = x_rows(d, part)
            gu = dot_l(tokb[:, at], guh[h]).astype(BF16)
            dn = dot_l(gob[:, at], hdup[h])
            dwq[h, d, 0], dwq[h, d, 1] = gu[:hp], gu[hp:]
            dwq[h, d, 2] = jnp.where(ld, dn[:hp], dn[hp:]).astype(BF16)

    def grads_out(h, c):
        x_far[h].append(halves_out(dwq.at[h, 2, c], farq.at[h, c], dwqr.at[h, c], 2))
        for d in (1, 3):
            x_d1[h][c] += halves_out(dwq.at[h, d, c], farq.at[h, c], dwqr.at[h, c], d)

    def grads_on(h, c):
        x_d1[h][c] += halves_on(lambda d: dwq.at[h, d, c], farq.at[h, c], dwqr.at[h, c], x_far[h][c])

    def send_z(h, c):
        for a in x_d1[h][c]:
            a.wait_recv()
        total = dwq[h, 0, c].astype(F32) + dwqr[h, c, 0].astype(F32) + dwqr[h, c, 1].astype(F32)
        zsend[h, c] = total.astype(BF16)
        return copy(zsend.at[h, c], zrecv.at[h, c], z_peer)

    for c in x_w:
        c.wait_recv()
    hidden_own(0, 3)
    for c in x_r[0]:
        c.wait_recv()
    hidden_other(0, 0, 3)
    for c in y_c:
        c.wait_recv()
    pass_on(4)
    hidden_other(0, 3, 4)
    pass_on(5)
    pass_far(4)
    grads_other(0)
    pass_far(5)
    grads_out(0, 0)
    hidden_own(3, 4)

    for c in x_r[1]:
        c.wait_recv()
    grads_on(0, 0)
    grads_out(0, 1)
    grads_out(0, 2)
    hidden_other(1, 0, NY)
    z_d = []
    lall = low((hp, hidden))
    for s in range(NX):
        d0, d1 = rd[0, pl.ds(s * hp, hp)].astype(F32), rd[1, pl.ds(s * hp, hp)].astype(F32)
        rdn[pl.ds(s * part, hp)] = jnp.where(lall, d0, swap(d1)).astype(BF16)
        rdn[pl.ds(s * part + hp, hp)] = jnp.where(lall, swap(d0), d1).astype(BF16)
    lfull = low((NY * rows, hidden))
    hsb[1] = jnp.where(lfull, hdup[0].astype(F32), hdup[1].astype(F32)).astype(BF16)

    hs = jnp.concatenate([hsb[0], hsb[1]], axis=1)
    gu = jnp.concatenate([gub[0], gub[1]], axis=1)
    y_far = []
    for s in range(NX):
        cols = pl.ds(s * part, part)
        lop[:, cols] = dot_t(hs, jnp.concatenate([wb[2, cols], rdn[cols]], axis=1)).astype(BF16)
        both = jnp.concatenate([wb[0, cols], wb[1, cols], rw[0, cols], rw[1, cols]], axis=1)
        gtp[:, cols] = dot_t(gu, both).astype(BF16)
        for n, buf in enumerate((lop, gtp)):
            for m, d in enumerate((1, 3)):
                r0 = m * half
                c = copy(buf.at[slot(2, r0, half), cols], far.at[n, m, :, cols], y_peer(d))
                y_far.append(c)
        if s == 0:
            z_d.append(send_z(0, 0))
        if s == 1:
            grads_on(0, 1)
            grads_on(0, 2)
    y_g = [copy(gst.at[PLACE[d]], gsr.at[NY - d - 1], y_peer(d)) for d in (2, 1, 3)]
    y_o = []
    for buf, dst in ((lop, lor), (gtp, gtr)):
        for m, d in enumerate((1, 3)):
            r0 = half - m * half
            y_o.append(copy(buf.at[slot(d, r0, half)], dst.at[m, pl.ds(r0, half)], y_peer(d)))
    z_d += [send_z(0, 1), send_z(0, 2)]
    grads_other(1)
    for c in range(3):
        grads_out(1, c)

    for d in (2, 1, 3, 0):
        at = x_rows(d, part)
        both = dot_l(tokb[:, at], gub[0]).astype(BF16)
        dwb[d, 0], dwb[d, 1] = both[:, :hidden], both[:, hidden:]
        dwb[d, 2] = dot_l(gob[:, at], hsb[0]).astype(BF16)
    for c in range(3):
        grads_on(1, c)
    z_d += [send_z(1, c) for c in range(3)]
    w_far, x_d0 = [], []
    for i in range(3):
        w_far.append(halves_out(dwb.at[2, i], farw.at[i], dwr.at[i], 2))
    for i in range(3):
        for d in (1, 3):
            x_d0 += halves_out(dwb.at[d, i], farw.at[i], dwr.at[i], d)

    for s in range(NX):
        cols = pl.ds(s * part, part)
        for n, (buf, dst) in enumerate(((lop, lor), (gtp, gtr))):
            for m, d in enumerate((1, 3)):
                r0 = m * half
                y_far[4 * s + 2 * n + m].wait_recv()
                at = slot(d, r0, half)
                buf[at, cols] = (buf[at, cols].astype(F32) + far[n, m, :, cols].astype(F32)).astype(BF16)
                y_o.append(copy(buf.at[at, cols], dst.at[m, pl.ds(r0, half), cols], y_peer(d)))
    for i in range(3):
        x_d0 += halves_on(lambda d: dwb.at[d, i], farw.at[i], dwr.at[i], w_far[i])
    outs = []
    for c in y_g + y_o[:4]:
        c.wait_recv()
    for s in range(NX):
        cols = pl.ds(s * part, part)
        for n, (buf, got, out) in enumerate(((lop, lor, lo), (gtp, gtr, gt))):
            for m in range(2):
                y_o[4 + 4 * s + 2 * n + m].wait_recv()
            total = buf[slot(0), cols].astype(F32) + got[0, :, cols].astype(F32) + got[1, :, cols].astype(F32)
            buf[slot(0), cols] = total.astype(BF16)
            c = pltpu.make_async_copy(buf.at[slot(0), cols], out.at[:, cols], out_sem.at[2 * s + n])
            c.start()
            outs.append(c)
    gs_sum = gst[0] + gsr[0] + gsr[1] + gsr[2]
    for k in range(ids.shape[0]):
        gs[k : k + 1] = jnp.sum(jnp.where(sub == ids[k : k + 1], gs_sum, 0.0), axis=0, keepdims=True)

    for c in x_d0:
        c.wait_recv()
    for i in range(3):
        dout[i] = dwb[0, i].astype(F32) + dwr[i, 0].astype(F32) + dwr[i, 1].astype(F32)
    for c in range(2):
        z_d[c].wait_recv()
        z_d[3 + c].wait_recv()
        at = pl.ds(c * hp, hp)
        p1, p2 = zrecv[0, c].astype(F32), zrecv[1, c].astype(F32)
        dout[0, at] += jnp.where(ld, p1, swap(p2))
        dout[1, at] += jnp.where(ld, swap(p1), p2)
    for i, out in enumerate((dg, du, dd)):
        if i == 2:
            z_d[2].wait_recv()
            z_d[5].wait_recv()
            q1, q2 = zrecv[0, 2].astype(F32), zrecv[1, 2].astype(F32)
            dout[2, pl.ds(0, hp)] += jnp.where(ld, q1, swap(q2))
            dout[2, pl.ds(hp, hp)] += jnp.where(ld, swap(q1), q2)
        c = pltpu.make_async_copy(dout.at[i], out, out_sem.at[2 * NX + i])
        c.start()
        outs.append(c)
    for c in made:
        c.wait_send()
    for c in outs:
        c.wait()


def hand_on(*refs):
    n = (len(refs) - 2) // 3
    held, sem = refs[2 * n : 3 * n], refs[-2:]
    into = [pltpu.make_async_copy(refs[i], held[i], sem[0].at[i]) for i in range(n)]
    out = [pltpu.make_async_copy(held[i], refs[n + i], sem[1].at[i]) for i in range(n)]
    for c in into:
        c.start()
    for i in range(n):
        into[i].wait()
        out[i].start()
    for c in out:
        c.wait()


def local(tokens, expert_ids, gate_scores, gate_weight, up_weight, down_weight, grad_out):
    rows, width = tokens.shape
    _, part, hidden = gate_weight.shape
    top = expert_ids.shape[1]
    experts = lax.axis_size("expert")
    all_rows, half, hp = NY * rows, rows // 2, part // 2
    vmem, hbm = pl.BlockSpec(memory_space=pltpu.VMEM), pl.BlockSpec(memory_space=pl.ANY)
    shape = jax.ShapeDtypeStruct
    v = pltpu.VMEM
    scratch = [
        v((all_rows, width), BF16),
        v((all_rows, width), BF16),
        v((NY, experts, rows), F32),
        v((2, all_rows, hidden), F32),
        v((3, width, hidden), BF16),
        v((2, 3, hp, hidden), BF16),
        v((2, width, hidden), BF16),
        v((2, width // 2, hidden), BF16),
        v((width, hidden), BF16),
        v((all_rows, 2 * hidden), F32),
        v((all_rows, hidden), F32),
        v((all_rows, hidden), F32),
        v((2, all_rows, 2 * hidden), BF16),
        v((2, all_rows, hidden), BF16),
        v((2, all_rows, hidden), BF16),
        v((2, all_rows, hidden), BF16),
        v((NY, experts, rows), F32),
        v((NY - 1, experts, rows), F32),
        v((NX, 3, part, hidden), BF16),
        v((3, 2, part, hidden), BF16),
        v((3, 2, hp, hidden), BF16),
        v((2, NX, 3, hp, hidden), BF16),
        v((2, 3, 2, hp, hidden), BF16),
        v((2, 3, 2, hp // 2, hidden), BF16),
        v((2, 3, hp, hidden), BF16),
        v((2, 3, hp, hidden), BF16),
        v((all_rows, width), BF16),
        v((all_rows, width), BF16),
        v((2, 2, half, width), BF16),
        v((2, rows, width), BF16),
        v((2, rows, width), BF16),
        v((3, part, hidden), F32),
        pltpu.SemaphoreType.DMA((N_COPIES,)),
        pltpu.SemaphoreType.DMA((N_COPIES,)),
        pltpu.SemaphoreType.DMA((5,)),
        pltpu.SemaphoreType.DMA((2 * NX + 3,)),
    ]
    big, weight = shape((rows, width), BF16), shape((part, hidden), F32)
    shapes = [big, big, shape((top, rows), F32), weight, weight, weight]
    outs = pl.pallas_call(
        kernel,
        out_shape=shapes,
        in_specs=[hbm, hbm, vmem, vmem, hbm, hbm, hbm],
        out_specs=[hbm, hbm, vmem, hbm, hbm, hbm],
        scratch_shapes=scratch,
        compiler_params=pltpu.CompilerParams(
            collective_id=0, has_side_effects=True, vmem_limit_bytes=60 << 20
        ),
    )(tokens, grad_out, expert_ids.T, gate_scores.T, gate_weight[0], up_weight[0], down_weight[0])
    lo, gt, gs, dg, du, dd = pl.pallas_call(
        hand_on,
        out_shape=shapes,
        in_specs=[hbm] * 6,
        out_specs=[hbm] * 6,
        scratch_shapes=[v(o.shape, o.dtype) for o in shapes] + [pltpu.SemaphoreType.DMA((6,))] * 2,
    )(*outs)
    return lo, gt, gs.T, dg[None], du[None], dd[None]


def solution(mesh):
    rows_p = P(("section", "expert", "dp"), None)
    weight_p = P(("section", "expert"), "dp", None)
    return jax.shard_map(
        local,
        mesh=mesh,
        in_specs=(rows_p, rows_p, rows_p, weight_p, weight_p, weight_p, rows_p),
        out_specs=(rows_p, rows_p, rows_p, weight_p, weight_p, weight_p),
        check_vma=False,
    )
```
